32 devices in a mesh: blk: 8 (over y, x, core), inner: 4 (over z).
Axes of the slice: x: 2, y: 2, z: 4, core: 2. Of those that a mesh axis runs over, the one named last changes fastest.
Arguments:
- records: float32 [1024, 16, 2048], P('blk', 'inner'), may hold values from -6 to 6
- starts: int32 [16], P('inner'), may hold values from 0 to 1024, as said below
- offsets: int32 [1024, 16], P('blk'), may hold values from -256 to 256, as said below
Outputs:
- correlations: float32 [16, 1024, 768], P('inner', 'blk')
The draws below stay inside these ranges and needn't reach their ends.
Inputs may be any that keep to these rules, and one draw needn't show every extreme that they name: Segment s uses samples starts[s] to starts[s] + 1023 of its slot. `offsets`: never zero; the partner of channel c is (c + offset) mod 1024.
All inputs are finite; a program needn't handle non-finite values.
Results may differ from the reference program's by a relative error of at most 0.0003.
Values sent between devices are 32-bit elements; how exact they have to be, the bound alone decides.
No kernel may reach another device: no remote copies, remote signals or barrier semaphores. Data moves between devices by JAX's collectives and lax.ppermute only.
A program may use at most 128 MiB of HBM per device.

```python
import math
import jax
import jax.numpy as jnp
from jax import lax

SEG = 1024
SLOT = 2048
LAGS = 768
HALF = 32
PAIRS = 16
F = 512
SEP = 256
CHANNELS = 1024
SEGS = 16


def draw_starts(key, part):
    values = jax.random.randint(key, (SEGS,), 0, SLOT - SEG + 1)
    values = values.at[0].set(0).at[1].set(SLOT - SEG)
    return values.astype(jnp.int32)


def draw_offsets(key, part):
    first_key, second_key = jax.random.split(key)
    magnitude = jax.random.randint(first_key, (CHANNELS, PAIRS), 1, SEP + 1)
    direction = jax.random.randint(second_key, (CHANNELS, PAIRS), 0, 2) * 2 - 1
    values = magnitude * direction
    values = values.at[0, 0].set(SEP).at[1, 0].set(-SEP)
    return values.astype(jnp.int32)


def steps_of(stream_key, shape, cuts, smallest, top_value):
    gain, own = 1.0, jax.random.fold_in(stream_key, 6)
    for position, shards_of in cuts:
        draws = jnp.exp(jax.random.uniform(jax.random.fold_in(own, position), (shards_of,), jnp.float32, smallest / len(cuts), top_value / len(cuts)))
        gain = gain * jnp.repeat(draws, shape[position] // shards_of).reshape([-1 if axis == position else 1 for axis in range(len(shape))])
    return gain


def gaussian(key, shape, width, most, cuts=(), held_as=jnp.bfloat16):
    values = width * jax.random.normal(key, shape, jnp.float32)
    if cuts:
        values = values * steps_of(key, shape, cuts, -0.22, 0.18)
    return jnp.clip(values, -most, most).astype(held_as)


def setup_inputs(seed: int = 0) -> dict:
    seeds = jax.random.split(jax.random.key(seed), 4)
    records = gaussian(seeds[0], (CHANNELS, SEGS, SLOT), 1.0, 6.0, ((0, 8), (1, 4)), jnp.float32)
    starts = draw_starts(jax.random.fold_in(seeds[3], 71), 0)
    offsets = draw_offsets(jax.random.fold_in(seeds[3], 71), 0)
    return {"records": records, "starts": starts, "offsets": offsets}


def lag_table():
    bins = jnp.arange(F, dtype=jnp.int32)
    shifts = jnp.arange(LAGS, dtype=jnp.int32) - LAGS // 2
    phase = bins[:, None] * shifts[None, :] % SEG
    angle = 2.0 * jnp.pi / SEG * phase.astype(jnp.float32)
    table = jnp.concatenate([jnp.cos(angle), -jnp.sin(angle)], 0)
    return (table * math.sqrt(SEGS / F)).astype(jnp.float32)

def reference(records, starts, offsets):
    samples = jnp.arange(SEG, dtype=jnp.int32).astype(jnp.float32)
    window = (0.5 - 0.5 * jnp.cos(2.0 * jnp.pi * samples / SEG)).astype(jnp.float32)
    bins = jnp.arange(F, dtype=jnp.int32)
    distance = jnp.abs(bins[:, None] - bins[None, :])
    distance = jnp.minimum(distance, F - distance)
    band = ((distance <= HALF).astype(jnp.float32) / (2 * HALF + 1)).astype(jnp.float32)

    def one_segment(inputs):
        slot_rows, begin = inputs
        pieces = lax.dynamic_slice_in_dim(slot_rows, begin.astype(jnp.int32), SEG, 1) * window
        spectrum = jnp.fft.rfft(pieces, axis=1)[:, :F]
        spec_re = jnp.real(spectrum).astype(jnp.float32)
        spec_im = jnp.imag(spectrum).astype(jnp.float32)
        power = spec_re * spec_re + spec_im * spec_im
        smooth = jnp.dot(power, band, precision=lax.Precision.HIGHEST, preferred_element_type=jnp.float32)
        scale = lax.rsqrt(smooth + 1e-06)
        return (spec_re * scale, spec_im * scale)
    white_re, white_im = lax.map(one_segment, (jnp.moveaxis(records, 1, 0), starts))
    table = lag_table()
    channel_ids = jnp.arange(CHANNELS, dtype=jnp.int32)

    def one_pair(column):
        partner = (channel_ids + offsets[:, column]) % CHANNELS
        partner_re = white_re[:, partner, :]
        partner_im = white_im[:, partner, :]
        cross_re = lax.optimization_barrier(jnp.sum(white_re * partner_re + white_im * partner_im, axis=0)) / SEGS
        cross_im = lax.optimization_barrier(jnp.sum(white_im * partner_re - white_re * partner_im, axis=0)) / SEGS
        joined = jnp.concatenate([cross_re, cross_im], 1)
        return jnp.dot(joined, table, precision=lax.Precision.HIGHEST, preferred_element_type=jnp.float32)
    return lax.map(one_pair, jnp.arange(PAIRS, dtype=jnp.int32))
```

```python
import functools
import math

import jax
import jax.numpy as jnp
import numpy as np
from jax import lax
from jax.experimental import pallas as pl
from jax.experimental.pallas import tpu as pltpu
from jax.sharding import PartitionSpec as P

SEG = 1024
LAGS = 768
HALF = 32
F = 512
LANES = 128
EPS = 1e-06


def bin_order():
    m = np.arange(128)
    return np.concatenate([4 * m, 4 * m + 2, 4 * m + 1, 4 * m[::-1] + 3])


def transform_tables():
    u = np.arange(256)

    def angle(bins):
        return 2 * np.pi / SEG * (bins[:, None] * u[None, :] % SEG)

    m = np.arange(128)
    even = [angle(4 * m), angle(4 * m + 2)]
    even = [np.concatenate([np.cos(a), -np.sin(a)], 0) for a in even]
    a = angle(4 * np.arange(256) + 1)
    sign = np.where(np.arange(256) < 128, 1.0, -1.0)[:, None]
    odd_re = np.concatenate([np.cos(a), -np.sin(a)], 1)
    odd_im = np.concatenate([-np.sin(a), -np.cos(a)], 1) * sign
    odd = np.concatenate([odd_re, odd_im], 0)
    return [t.astype(np.float32) for t in (even[0], even[1], odd)]


def band_table():
    order = bin_order()
    distance = np.abs(order[:, None] - order[None, :])
    distance = np.minimum(distance, F - distance)
    return (distance <= HALF).astype(np.float32)


def lag_table(width, segment_count):
    shifts = np.arange(LAGS) - LAGS // 2
    angle = 2 * np.pi / SEG * (bin_order()[:, None] * shifts[None, :] % SEG)
    table = np.stack([np.cos(angle), -np.sin(angle)], 0).reshape(2, F // width, width, LAGS)
    factor = math.sqrt(segment_count / F) / segment_count
    return (table.transpose(1, 0, 2, 3).reshape(2 * F, LAGS) * factor).astype(np.float32)


def halves(x):
    high = x.astype(jnp.bfloat16)
    return high, (x - high.astype(jnp.float32)).astype(jnp.bfloat16)


def dot_nt(a, b, precision=None):
    return lax.dot_general(
        a, b, (((1,), (1,)), ((), ())), precision=precision, preferred_element_type=jnp.float32
    )


def dot_tn(a, b):
    return lax.dot_general(a, b, (((0,), (0,)), ((), ())), preferred_element_type=jnp.float32)


def whiten_kernel(records_ref, window_ref, even0_ref, even2_ref, odd_ref, band_ref, out_ref):
    count = records_ref.shape[1]
    rows = out_ref.shape[3]
    sums, alternating, odds = [], [], []
    for s in range(count):
        folded = records_ref[:, s, :SEG] * window_ref[s : s + 1, :SEG]
        folded += records_ref[:, s, SEG:] * window_ref[s : s + 1, SEG:]
        x = [folded[:, 256 * j : 256 * (j + 1)] for j in range(4)]
        sums.append((x[0] + x[2]) + (x[1] + x[3]))
        alternating.append((x[0] + x[2]) - (x[1] + x[3]))
        odds.append(jnp.concatenate([x[0] - x[2], x[1] - x[3]], 1))
    highest = lax.Precision.HIGHEST
    s0 = dot_nt(even0_ref[...], jnp.concatenate(sums, 0), highest)
    s2 = dot_nt(even2_ref[...], jnp.concatenate(alternating, 0), highest)
    s1 = dot_nt(odd_ref[...], jnp.concatenate(odds, 0), highest)
    re = jnp.concatenate([s0[:128], s2[:128], s1[:256]], 0)
    im = jnp.concatenate([s0[128:], s2[128:], s1[256:]], 0)
    high, low = halves(re * re + im * im)
    band = band_ref[...]
    smooth = jnp.dot(band, high, preferred_element_type=jnp.float32)
    smooth += jnp.dot(band, low, preferred_element_type=jnp.float32)
    scale = lax.rsqrt(smooth * (1.0 / (2 * HALF + 1)) + EPS)
    re, im = re * scale, im * scale
    for s in range(count):
        lanes = slice(s * LANES, (s + 1) * LANES)
        out_ref[:, s, 0] = re[:, lanes].reshape(-1, rows, LANES)
        out_ref[:, s, 1] = im[:, lanes].reshape(-1, rows, LANES)


def whiten(records, starts, rows):
    count = records.shape[1]
    samples = jnp.arange(SEG, dtype=jnp.int32)[None, :]
    begin = starts[:, None].astype(jnp.int32)
    phase = (samples - begin) % SEG
    window = 0.5 - 0.5 * jnp.cos(2.0 * jnp.pi / SEG * phase.astype(jnp.float32))
    early = samples >= begin
    window = jnp.concatenate([jnp.where(early, window, 0.0), jnp.where(early, 0.0, window)], 1)
    tables = [jnp.asarray(t) for t in transform_tables()]
    band = jnp.asarray(band_table(), jnp.bfloat16)
    return pl.pallas_call(
        whiten_kernel,
        out_shape=jax.ShapeDtypeStruct((F // rows, count, 2, rows, LANES), jnp.float32),
        compiler_params=pltpu.CompilerParams(vmem_limit_bytes=56 << 20),
    )(records, window, *tables, band)


def pair_kernel(index_ref, spectra_ref, sum_ref, out_ref, wide_ref, product_ref, *, width):
    block = pl.program_id(0)
    blocks, depth = spectra_ref.shape[:2]
    pairs = index_ref.shape[1]
    groups = out_ref.shape[1]
    share = pairs // groups

    @pl.when(block == 0)
    def _():
        if depth < 4:
            wide_ref[...] = jnp.zeros(wide_ref.shape, wide_ref.dtype)

        def build(i, carry):
            for r in range(depth):
                turned = spectra_ref[i, r].T
                for h in range(2):
                    wide_ref[pl.ds(i * 8 * LANES + 2 * r + h, LANES, stride=8), :] = turned
            return carry

        lax.fori_loop(0, blocks, build, 0)

    row = lax.broadcasted_iota(jnp.int32, (8, LANES), 0)
    lane = lax.broadcasted_iota(jnp.int32, (8, LANES), 1)
    bit0, bit1, bit2 = row % 2 == 0, row // 2 % 2 == 0, row // 4 == 0
    is_re = lane // width % 2 == 0

    def roll(x, steps):
        return pltpu.roll(x, steps % 8, 0)

    def fold4(a, b):
        return jnp.where(bit2, a, b) + roll(jnp.where(bit2, b, a), 4)

    def fold2(a, b):
        return jnp.where(bit1, a + roll(a, -2), b + roll(b, 2))

    def group(g, carry):
        first = pl.multiple_of(g * 8, 8)
        own = []
        for j in range(8):
            at = pl.multiple_of((block * LANES + first + j) * 8, 8)
            w = wide_ref[pl.ds(at, 8), :]
            turned = jnp.where(is_re, pltpu.roll(w, LANES - width, 1), -pltpu.roll(w, width, 1))
            own.append(jnp.where(bit0, w, turned))
        for k in range(pairs):
            p = []
            for j in range(8):
                at = pl.multiple_of(index_ref[0, k, first + j], 8)
                p.append(own[j] * wide_ref[pl.ds(at, 8), :])
            even = fold2(fold4(p[0], p[4]), fold4(p[2], p[6]))
            odd = fold2(fold4(p[1], p[5]), fold4(p[3], p[7]))
            product_ref[0, k, pl.ds(first, 8), :] = jnp.where(bit0, even, roll(odd, 1))
            product_ref[1, k, pl.ds(first, 8), :] = jnp.where(bit0, roll(even, -1), odd)
        return carry

    lax.fori_loop(0, LANES // 8, group, 0)
    for z in range(groups):
        for h in range(2):
            x = product_ref[h, z * share : (z + 1) * share].reshape(share * LANES, LANES)
            out_ref[0, z, h] = dot_nt(sum_ref[...], jnp.concatenate(halves(x), 1))


def pair_products(spectra, index, groups, width):
    blocks = spectra.shape[0]
    pairs = index.shape[1]
    rows = max(width, 8)
    summing = np.zeros((rows, LANES), np.float32)
    summing[np.arange(LANES) % width, np.arange(LANES)] = 1
    summing = jnp.asarray(np.concatenate([summing, summing], 1), jnp.bfloat16)
    shape = (groups, 2, rows, pairs // groups * LANES)
    return pl.pallas_call(
        functools.partial(pair_kernel, width=width),
        grid=(blocks,),
        in_specs=[
            pl.BlockSpec((1, pairs, LANES), lambda b: (b, 0, 0), memory_space=pltpu.SMEM),
            pl.BlockSpec(spectra.shape, lambda b: (0,) * 4),
            pl.BlockSpec(summing.shape, lambda b: (0, 0)),
        ],
        out_specs=pl.BlockSpec((1, *shape), lambda b: (b, 0, 0, 0, 0)),
        out_shape=jax.ShapeDtypeStruct((blocks, *shape), jnp.float32),
        scratch_shapes=[
            pltpu.VMEM((blocks * LANES * 8, LANES), jnp.float32),
            pltpu.VMEM((2, pairs, LANES, LANES), jnp.float32),
        ],
        compiler_params=pltpu.CompilerParams(vmem_limit_bytes=56 << 20),
    )(index, spectra, summing)


def lag_kernel(cross_ref, high_ref, low_ref, out_ref):
    high, low = halves(cross_ref[...])
    total = dot_tn(high, low_ref[...]) + dot_tn(low, high_ref[...])
    out_ref[0] = total + dot_tn(high, high_ref[...])


def lag_transform(cross, table):
    count = cross.shape[1] // LANES
    high = table.astype(jnp.bfloat16)
    low = (table - high.astype(np.float32)).astype(jnp.bfloat16)
    return pl.pallas_call(
        lag_kernel,
        grid=(count,),
        in_specs=[
            pl.BlockSpec((2 * F, LANES), lambda i: (0, i)),
            pl.BlockSpec((2 * F, LAGS), lambda i: (0, 0)),
            pl.BlockSpec((2 * F, LAGS), lambda i: (0, 0)),
        ],
        out_specs=pl.BlockSpec((1, LANES, LAGS), lambda i: (i, 0, 0)),
        out_shape=jax.ShapeDtypeStruct((count, LANES, LAGS), jnp.float32),
        compiler_params=pltpu.CompilerParams(vmem_limit_bytes=56 << 20),
    )(cross, jnp.asarray(high), jnp.asarray(low))


def local(records, starts, offsets):
    axes = ("blk", "inner")
    blocks, groups = lax.axis_size("blk"), lax.axis_size("inner")
    devices = blocks * groups
    width = F // devices
    here, count = records.shape[:2]
    channels = here * blocks
    ids = jnp.arange(here, dtype=jnp.int32)[:, None] + lax.axis_index("blk") * here
    index = (((ids + offsets) % channels) * 8).T
    index = lax.all_gather(index, "blk", axis=0)
    rows = max(width, 8)
    white = whiten(records, starts, rows)
    split = rows // width
    white = white.reshape(-1, count, 2, split, width, LANES).transpose(0, 3, 1, 2, 4, 5)
    white = white.reshape(devices, count * 2 * width, LANES)
    spectra = lax.all_to_all(white, axes, 0, 0, tiled=True)
    spectra = spectra.reshape(blocks, -1, LANES, LANES)
    cross = pair_products(spectra, index, groups, width)
    cross = cross[:, :, :, :width].reshape(devices, 2 * width, -1)
    cross = lax.all_to_all(cross, axes, 0, 0, tiled=True)
    return lag_transform(cross.reshape(2 * F, -1), lag_table(width, count * groups))


def solution(mesh):
    placed = (P("blk", "inner", None), P("inner"), P("blk", None))
    return jax.shard_map(
        local, mesh=mesh, in_specs=placed, out_specs=P("inner", "blk", None), check_vma=False
    )
```

```python
import functools
import math

import jax
import jax.numpy as jnp
import numpy as np
from jax import lax
from jax.experimental import pallas as pl
from jax.experimental.pallas import tpu as pltpu
from jax.sharding import PartitionSpec as P

SEG = 1024
LAGS = 768
HALF = 32
REACH = 256
F = 512
LANES = 128
EPS = 1e-06


def bin_order():
    m = np.arange(128)
    return np.concatenate([4 * m, 4 * m + 2, 4 * m + 1, 4 * m[::-1] + 3])


def transform_tables():
    u = np.arange(256)

    def angle(bins):
        return 2 * np.pi / SEG * (bins[:, None] * u[None, :] % SEG)

    m = np.arange(128)
    even = [angle(4 * m), angle(4 * m + 2)]
    even = [np.concatenate([np.cos(a), -np.sin(a)], 0) for a in even]
    a = angle(4 * np.arange(256) + 1)
    sign = np.where(np.arange(256) < 128, 1.0, -1.0)[:, None]
    odd_re = np.concatenate([np.cos(a), -np.sin(a)], 1)
    odd_im = np.concatenate([-np.sin(a), -np.cos(a)], 1) * sign
    odd = np.concatenate([odd_re, odd_im], 0)
    return [t.astype(np.float32) for t in (even[0], even[1], odd)]


def band_table():
    order = bin_order()
    distance = np.abs(order[:, None] - order[None, :])
    distance = np.minimum(distance, F - distance)
    return (distance <= HALF).astype(np.float32)


def lag_table(width, segment_count):
    shifts = np.arange(LAGS) - LAGS // 2
    angle = 2 * np.pi / SEG * (bin_order()[:, None] * shifts[None, :] % SEG)
    table = np.stack([np.cos(angle), -np.sin(angle)], 0).reshape(2, F // width, width, LAGS)
    factor = math.sqrt(segment_count / F) / segment_count
    return (table.transpose(1, 0, 2, 3).reshape(2 * F, LAGS) * factor).astype(np.float32)


def halves(x):
    high = x.astype(jnp.bfloat16)
    return high, (x - high.astype(jnp.float32)).astype(jnp.bfloat16)


def dot_nt(a, b, precision=None):
    return lax.dot_general(
        a, b, (((1,), (1,)), ((), ())), precision=precision, preferred_element_type=jnp.float32
    )


def dot_tn(a, b):
    return lax.dot_general(a, b, (((0,), (0,)), ((), ())), preferred_element_type=jnp.float32)


def hann_table():
    window = 0.5 - 0.5 * np.cos(2 * np.pi / SEG * np.arange(SEG))
    return np.tile(window[None, :], (8, 1)).astype(np.float32)


def whiten_kernel(
    starts_ref, records_ref, hann_ref, even0_ref, even2_ref, odd_ref, band_ref, out_ref, folded_ref
):
    step = pl.program_id(0)
    part, count = records_ref.shape[:2]
    rows = out_ref.shape[3]
    place = pl.multiple_of(step * part, part)
    samples = lax.broadcasted_iota(jnp.int32, (8, SEG), 1)
    for s in range(count):
        begin = starts_ref[s]
        window = pltpu.roll(hann_ref[...], lax.rem(begin, SEG), 1)[:1]
        early = jnp.where(samples >= begin, 1.0, 0.0)[:1] * window
        late = window - early
        x = records_ref[:, s, :SEG] * early + records_ref[:, s, SEG:] * late
        x = [x[:, 256 * j : 256 * (j + 1)] for j in range(4)]
        at = pl.ds(s * LANES + place, part)
        folded_ref[at, :256] = (x[0] + x[2]) + (x[1] + x[3])
        folded_ref[at, 256:512] = (x[0] + x[2]) - (x[1] + x[3])
        folded_ref[at, 512:768] = x[0] - x[2]
        folded_ref[at, 768:] = x[1] - x[3]

    @pl.when(step == pl.num_programs(0) - 1)
    def _():
        highest = lax.Precision.HIGHEST
        s0 = dot_nt(even0_ref[...], folded_ref[:, :256], highest)
        s2 = dot_nt(even2_ref[...], folded_ref[:, 256:512], highest)
        s1 = dot_nt(odd_ref[...], folded_ref[:, 512:], highest)
        re = jnp.concatenate([s0[:128], s2[:128], s1[:256]], 0)
        im = jnp.concatenate([s0[128:], s2[128:], s1[256:]], 0)
        high, low = halves(re * re + im * im)
        band = band_ref[...]
        smooth = jnp.dot(band, high, preferred_element_type=jnp.float32)
        smooth += jnp.dot(band, low, preferred_element_type=jnp.float32)
        scale = lax.rsqrt(smooth * (1.0 / (2 * HALF + 1)) + EPS)
        re, im = re * scale, im * scale
        for s in range(count):
            lanes = slice(s * LANES, (s + 1) * LANES)
            out_ref[:, s, 0] = re[:, lanes].reshape(-1, rows, LANES)
            out_ref[:, s, 1] = im[:, lanes].reshape(-1, rows, LANES)


def whiten(records, starts, rows):
    here, count, slot = records.shape
    part = 32
    tables = [jnp.asarray(t) for t in (hann_table(), *transform_tables())]
    tables.append(jnp.asarray(band_table(), jnp.bfloat16))
    shape = (F // rows, count, 2, rows, LANES)
    return pl.pallas_call(
        whiten_kernel,
        grid=(here // part,),
        in_specs=[
            pl.BlockSpec(memory_space=pltpu.SMEM),
            pl.BlockSpec((part, count, slot), lambda i: (i, 0, 0)),
            *[pl.BlockSpec(memory_space=pltpu.VMEM) for _ in tables],
        ],
        out_specs=pl.BlockSpec(shape, lambda i: (0,) * 5),
        out_shape=jax.ShapeDtypeStruct(shape, jnp.float32),
        scratch_shapes=[pltpu.VMEM((count * LANES, SEG), jnp.float32)],
        compiler_params=pltpu.CompilerParams(vmem_limit_bytes=32 << 20),
    )(starts, records, *tables)


def pair_kernel(index_ref, spectra_ref, out_ref, wide_ref, hot_ref, *, reach, turned):
    block = pl.program_id(0)
    blocks, terms, _, rows, _ = spectra_ref.shape
    pairs = index_ref.shape[1]
    groups = out_ref.shape[1]
    share = pairs // groups
    span = 2 * reach + 1

    @pl.when(block == 0)
    def _():
        def build(i, carry):
            wide_ref[i, 0], wide_ref[i, 1] = halves(spectra_ref[i].reshape(-1, LANES))
            return carry

        lax.fori_loop(0, blocks, build, 0)

    near = [lax.rem(block + (blocks - reach + j), blocks) for j in range(span)]
    left = jnp.concatenate([wide_ref[i, h] for i in near for h in range(2)], 1)
    ids = lax.broadcasted_iota(jnp.int32, (LANES, LANES), 0)

    def put(k, h, rows_here, x):
        z, q = k // share, k % share
        out_ref[0, z, h, rows_here, q * LANES : (q + 1) * LANES] = x

    def by_product(n, ks):
        for i, k in enumerate(ks):
            row = index_ref[0, k : k + 1, :]
            for j in range(span):
                hot = jnp.where(ids + j * LANES == row, 1.0, 0.0).astype(jnp.bfloat16)
                for h in range(2):
                    at = (2 * j + h) * LANES
                    hot_ref[n % 2, at : at + LANES, i * LANES : (i + 1) * LANES] = hot
        found = jnp.dot(
            left, hot_ref[n % 2, :, : len(ks) * LANES], preferred_element_type=jnp.float32
        )
        found = found.reshape(terms, 2, rows, -1)
        for i, k in enumerate(ks):
            lanes = slice(i * LANES, (i + 1) * LANES)
            re = im = 0
            for t in range(terms):
                partner_re, partner_im = found[t, 0, :, lanes], found[t, 1, :, lanes]
                own_re, own_im = spectra_ref[block, t, 0], spectra_ref[block, t, 1]
                re = re + (own_re * partner_re + own_im * partner_im)
                im = im + (own_im * partner_re - own_re * partner_im)
            put(k, 0, slice(0, rows), re)
            put(k, 1, slice(0, rows), im)

    def by_gather(k, first):
        row = jnp.broadcast_to(index_ref[0, k : k + 1, :], (8, LANES))
        lane, part = row & (LANES - 1), lax.shift_right_logical(row, 7)
        rows_here = slice(first, first + 8)
        re = im = 0
        for t in range(terms):
            partner = []
            for h in range(2):
                found = jnp.take_along_axis(spectra_ref[near[0], t, h, rows_here], lane, axis=1)
                for j in range(1, span):
                    other = jnp.take_along_axis(spectra_ref[near[j], t, h, rows_here], lane, axis=1)
                    found = jnp.where(part == j, other, found)
                partner.append(found)
            own_re = spectra_ref[block, t, 0, rows_here]
            own_im = spectra_ref[block, t, 1, rows_here]
            re = re + (own_re * partner[0] + own_im * partner[1])
            im = im + (own_im * partner[0] - own_re * partner[1])
        put(k, 0, rows_here, re)
        put(k, 1, rows_here, im)

    chunks = [range(k, min(k + 2, pairs - turned)) for k in range(0, pairs - turned, 2)]
    gathers = [(k, first) for k in range(pairs - turned, pairs) for first in range(0, rows, 8)]
    for n, ks in enumerate(chunks):
        by_product(n, ks)
        for k, first in gathers[n * len(gathers) // len(chunks) : (n + 1) * len(gathers) // len(chunks)]:
            by_gather(k, first)


def pair_products(spectra, index, groups, turned=6):
    blocks, terms, _, rows, _ = spectra.shape
    pairs = index.shape[1]
    reach = -(-REACH // LANES)
    shape = (groups, 2, rows, pairs // groups * LANES)
    return pl.pallas_call(
        functools.partial(pair_kernel, reach=reach, turned=turned),
        grid=(blocks,),
        in_specs=[
            pl.BlockSpec((1, pairs, LANES), lambda b: (b, 0, 0)),
            pl.BlockSpec(memory_space=pltpu.VMEM),
        ],
        out_specs=pl.BlockSpec((1, *shape), lambda b: (b, 0, 0, 0, 0)),
        out_shape=jax.ShapeDtypeStruct((blocks, *shape), jnp.float32),
        scratch_shapes=[
            pltpu.VMEM((blocks, 2, terms * 2 * rows, LANES), jnp.bfloat16),
            pltpu.VMEM((2, 2 * (2 * reach + 1) * LANES, 2 * LANES), jnp.bfloat16),
        ],
        compiler_params=pltpu.CompilerParams(vmem_limit_bytes=32 << 20),
    )(index, spectra)


def lag_kernel(cross_ref, high_ref, low_ref, out_ref):
    high, low = halves(cross_ref[...])
    total = dot_tn(high, low_ref[...]) + dot_tn(low, high_ref[...])
    out_ref[0] = total + dot_tn(high, high_ref[...])


def lag_transform(cross, table):
    count = cross.shape[1] // LANES
    high = table.astype(jnp.bfloat16)
    low = (table - high.astype(np.float32)).astype(jnp.bfloat16)
    return pl.pallas_call(
        lag_kernel,
        grid=(count,),
        in_specs=[
            pl.BlockSpec((2 * F, LANES), lambda i: (0, i)),
            pl.BlockSpec(memory_space=pltpu.VMEM),
            pl.BlockSpec(memory_space=pltpu.VMEM),
        ],
        out_specs=pl.BlockSpec((1, LANES, LAGS), lambda i: (i, 0, 0)),
        out_shape=jax.ShapeDtypeStruct((count, LANES, LAGS), jnp.float32),
        compiler_params=pltpu.CompilerParams(vmem_limit_bytes=32 << 20),
    )(cross, jnp.asarray(high), jnp.asarray(low))


def local(records, starts, offsets):
    axes = ("blk", "inner")
    blocks, groups = lax.axis_size("blk"), lax.axis_size("inner")
    devices = blocks * groups
    width = F // devices
    here, count = records.shape[:2]
    ids = jnp.arange(here, dtype=jnp.int32)[:, None] + REACH
    index = lax.all_gather((ids + offsets).T, "blk", axis=0)
    rows = max(width, 8)
    split = rows // width
    white = whiten(records, starts, rows)
    white = white.reshape(-1, count // split, split, 2, split, width, LANES)
    white = white.transpose(0, 4, 1, 3, 2, 5, 6).reshape(devices, -1, LANES)
    spectra = lax.all_to_all(white, axes, 0, 0, tiled=True)
    spectra = spectra.reshape(blocks, -1, 2, rows, LANES)
    cross = pair_products(spectra, index, groups)
    if split > 1:
        cross = cross.reshape(blocks, groups, 2, split, width, -1).sum(3)
    cross = lax.all_to_all(cross.reshape(devices, 2 * width, -1), axes, 0, 0, tiled=True)
    return lag_transform(cross.reshape(2 * F, -1), lag_table(width, count * groups))


def solution(mesh):
    placed = (P("blk", "inner", None), P("inner"), P("blk", None))
    return jax.shard_map(
        local, mesh=mesh, in_specs=placed, out_specs=P("inner", "blk", None), check_vma=False
    )
```

```python
import functools
import math

import jax
import jax.numpy as jnp
import numpy as np
from jax import lax
from jax.experimental import pallas as pl
from jax.experimental.pallas import tpu as pltpu
from jax.sharding import PartitionSpec as P

SEG = 1024
LAGS = 768
HALF = 32
REACH = 256
F = 512
LANES = 128
EPS = 1e-06


def bin_order():
    m = np.arange(128)
    return np.concatenate([4 * m, 4 * m + 2, 4 * m + 1, 4 * m[::-1] + 3])


def transform_tables():
    u = np.arange(256)

    def angle(bins):
        return 2 * np.pi / SEG * (bins[:, None] * u[None, :] % SEG)

    m = np.arange(128)
    even = [angle(4 * m), angle(4 * m + 2)]
    even = [np.concatenate([np.cos(a), -np.sin(a)], 0) for a in even]
    a = angle(4 * np.arange(256) + 1)
    sign = np.where(np.arange(256) < 128, 1.0, -1.0)[:, None]
    odd_re = np.concatenate([np.cos(a), -np.sin(a)], 1)
    odd_im = np.concatenate([-np.sin(a), -np.cos(a)], 1) * sign
    odd = np.concatenate([odd_re, odd_im], 0)
    return [t.astype(np.float32) for t in (even[0], even[1], odd)]


def band_table():
    order = bin_order()
    distance = np.abs(order[:, None] - order[None, :])
    distance = np.minimum(distance, F - distance)
    return (distance <= HALF).astype(np.float32)


def lag_table(width, segment_count):
    shifts = np.arange(LAGS) - LAGS // 2
    angle = 2 * np.pi / SEG * (bin_order()[:, None] * shifts[None, :] % SEG)
    table = np.stack([np.cos(angle), -np.sin(angle)], 0).reshape(2, F // width, width, LAGS)
    factor = math.sqrt(segment_count / F) / segment_count
    return (table.transpose(1, 0, 2, 3).reshape(2 * F, LAGS) * factor).astype(np.float32)


def halves(x):
    high = x.astype(jnp.bfloat16)
    return high, (x - high.astype(jnp.float32)).astype(jnp.bfloat16)


def dot_nt(a, b, precision=None):
    return lax.dot_general(
        a, b, (((1,), (1,)), ((), ())), precision=precision, preferred_element_type=jnp.float32
    )


def dot_tn(a, b):
    return lax.dot_general(a, b, (((0,), (0,)), ((), ())), preferred_element_type=jnp.float32)


def hann_table():
    window = 0.5 - 0.5 * np.cos(2 * np.pi / SEG * np.arange(SEG))
    return np.tile(window[None, :], (8, 1)).astype(np.float32)


def whiten_kernel(
    starts_ref, records_ref, hann_ref, even0_ref, even2_ref, odd_ref, band_ref, out_ref, folded_ref
):
    step = pl.program_id(0)
    part, count = records_ref.shape[:2]
    rows = out_ref.shape[3]
    place = pl.multiple_of(step * part, part)
    samples = lax.broadcasted_iota(jnp.int32, (8, SEG), 1)
    for s in range(count):
        begin = starts_ref[s]
        window = pltpu.roll(hann_ref[...], lax.rem(begin, SEG), 1)[:1]
        early = jnp.where(samples >= begin, 1.0, 0.0)[:1] * window
        late = window - early
        x = records_ref[:, s, :SEG] * early + records_ref[:, s, SEG:] * late
        x = [x[:, 256 * j : 256 * (j + 1)] for j in range(4)]
        at = pl.ds(s * LANES + place, part)
        folded_ref[at, :256] = (x[0] + x[2]) + (x[1] + x[3])
        folded_ref[at, 256:512] = (x[0] + x[2]) - (x[1] + x[3])
        folded_ref[at, 512:768] = x[0] - x[2]
        folded_ref[at, 768:] = x[1] - x[3]

    @pl.when(step == pl.num_programs(0) - 1)
    def _():
        highest = lax.Precision.HIGHEST
        s0 = dot_nt(even0_ref[...], folded_ref[:, :256], highest)
        s2 = dot_nt(even2_ref[...], folded_ref[:, 256:512], highest)
        s1 = dot_nt(odd_ref[...], folded_ref[:, 512:], highest)
        re = jnp.concatenate([s0[:128], s2[:128], s1[:256]], 0)
        im = jnp.concatenate([s0[128:], s2[128:], s1[256:]], 0)
        high, low = halves(re * re + im * im)
        band = band_ref[...]
        smooth = jnp.dot(band, high, preferred_element_type=jnp.float32)
        smooth += jnp.dot(band, low, preferred_element_type=jnp.float32)
        scale = lax.rsqrt(smooth * (1.0 / (2 * HALF + 1)) + EPS)
        re, im = re * scale, im * scale
        for s in range(count):
            lanes = slice(s * LANES, (s + 1) * LANES)
            out_ref[:, s, 0] = re[:, lanes].reshape(-1, rows, LANES)
            out_ref[:, s, 1] = im[:, lanes].reshape(-1, rows, LANES)


def whiten(records, starts, rows):
    here, count, slot = records.shape
    part = 32
    tables = [jnp.asarray(t) for t in (hann_table(), *transform_tables())]
    tables.append(jnp.asarray(band_table(), jnp.bfloat16))
    shape = (F // rows, count, 2, rows, LANES)
    return pl.pallas_call(
        whiten_kernel,
        grid=(here // part,),
        in_specs=[
            pl.BlockSpec(memory_space=pltpu.SMEM),
            pl.BlockSpec((part, count, slot), lambda i: (i, 0, 0)),
            *[pl.BlockSpec(t.shape, lambda i: (0, 0)) for t in tables],
        ],
        out_specs=pl.BlockSpec(shape, lambda i: (0,) * 5),
        out_shape=jax.ShapeDtypeStruct(shape, jnp.float32),
        scratch_shapes=[pltpu.VMEM((count * LANES, SEG), jnp.float32)],
        compiler_params=pltpu.CompilerParams(vmem_limit_bytes=56 << 20),
    )(starts, records, *tables)


def pair_kernel(index_ref, spectra_ref, out_ref, wide_ref, hot_ref, *, reach, turned):
    block = pl.program_id(0)
    blocks, terms, _, rows, _ = spectra_ref.shape
    pairs = index_ref.shape[1]
    groups = out_ref.shape[1]
    share = pairs // groups
    span = 2 * reach + 1

    @pl.when(block == 0)
    def _():
        def build(i, carry):
            wide_ref[i, 0], wide_ref[i, 1] = halves(spectra_ref[i].reshape(-1, LANES))
            return carry

        lax.fori_loop(0, blocks, build, 0)

    near = [lax.rem(block + (blocks - reach + j), blocks) for j in range(span)]
    left = jnp.concatenate([wide_ref[i, h] for i in near for h in range(2)], 1)
    ids = lax.broadcasted_iota(jnp.int32, (LANES, LANES), 0)

    def put(k, h, rows_here, x):
        z, q = k // share, k % share
        out_ref[0, z, h, rows_here, q * LANES : (q + 1) * LANES] = x

    def by_product(n, ks):
        for i, k in enumerate(ks):
            row = index_ref[0, k : k + 1, :]
            for j in range(span):
                hot = jnp.where(ids + j * LANES == row, 1.0, 0.0).astype(jnp.bfloat16)
                for h in range(2):
                    at = (2 * j + h) * LANES
                    hot_ref[n % 2, at : at + LANES, i * LANES : (i + 1) * LANES] = hot
        found = jnp.dot(
            left, hot_ref[n % 2, :, : len(ks) * LANES], preferred_element_type=jnp.float32
        )
        found = found.reshape(terms, 2, rows, -1)
        for i, k in enumerate(ks):
            lanes = slice(i * LANES, (i + 1) * LANES)
            re = im = 0
            for t in range(terms):
                partner_re, partner_im = found[t, 0, :, lanes], found[t, 1, :, lanes]
                own_re, own_im = spectra_ref[block, t, 0], spectra_ref[block, t, 1]
                re = re + (own_re * partner_re + own_im * partner_im)
                im = im + (own_im * partner_re - own_re * partner_im)
            put(k, 0, slice(0, rows), re)
            put(k, 1, slice(0, rows), im)

    def by_gather(k, first):
        row = jnp.broadcast_to(index_ref[0, k : k + 1, :], (8, LANES))
        lane, part = row & (LANES - 1), lax.shift_right_logical(row, 7)
        rows_here = slice(first, first + 8)
        re = im = 0
        for t in range(terms):
            partner = []
            for h in range(2):
                found = jnp.take_along_axis(spectra_ref[near[0], t, h, rows_here], lane, axis=1)
                for j in range(1, span):
                    other = jnp.take_along_axis(spectra_ref[near[j], t, h, rows_here], lane, axis=1)
                    found = jnp.where(part == j, other, found)
                partner.append(found)
            own_re = spectra_ref[block, t, 0, rows_here]
            own_im = spectra_ref[block, t, 1, rows_here]
            re = re + (own_re * partner[0] + own_im * partner[1])
            im = im + (own_im * partner[0] - own_re * partner[1])
        put(k, 0, rows_here, re)
        put(k, 1, rows_here, im)

    chunks = [range(k, min(k + 2, pairs - turned)) for k in range(0, pairs - turned, 2)]
    gathers = [(k, first) for k in range(pairs - turned, pairs) for first in range(0, rows, 8)]
    for n, ks in enumerate(chunks):
        by_product(n, ks)
        for k, first in gathers[n * len(gathers) // len(chunks) : (n + 1) * len(gathers) // len(chunks)]:
            by_gather(k, first)


def pair_products(spectra, index, groups, turned=6):
    blocks, terms, _, rows, _ = spectra.shape
    pairs = index.shape[1]
    reach = -(-REACH // LANES)
    shape = (groups, 2, rows, pairs // groups * LANES)
    return pl.pallas_call(
        functools.partial(pair_kernel, reach=reach, turned=turned),
        grid=(blocks,),
        in_specs=[
            pl.BlockSpec((1, pairs, LANES), lambda b: (b, 0, 0)),
            pl.BlockSpec(memory_space=pltpu.VMEM),
        ],
        out_specs=pl.BlockSpec((1, *shape), lambda b: (b, 0, 0, 0, 0)),
        out_shape=jax.ShapeDtypeStruct((blocks, *shape), jnp.float32),
        scratch_shapes=[
            pltpu.VMEM((blocks, 2, terms * 2 * rows, LANES), jnp.bfloat16),
            pltpu.VMEM((2, 2 * (2 * reach + 1) * LANES, 2 * LANES), jnp.bfloat16),
        ],
        compiler_params=pltpu.CompilerParams(vmem_limit_bytes=32 << 20),
    )(index, spectra)


def lag_kernel(cross_ref, high_ref, low_ref, out_ref):
    high, low = halves(cross_ref[...])
    total = dot_tn(high, low_ref[...]) + dot_tn(low, high_ref[...])
    out_ref[0] = total + dot_tn(high, high_ref[...])


def lag_transform(cross, table):
    count = cross.shape[1] // LANES
    high = table.astype(jnp.bfloat16)
    low = (table - high.astype(np.float32)).astype(jnp.bfloat16)
    return pl.pallas_call(
        lag_kernel,
        grid=(count,),
        in_specs=[
            pl.BlockSpec((2 * F, LANES), lambda i: (0, i)),
            pl.BlockSpec(memory_space=pltpu.VMEM),
            pl.BlockSpec(memory_space=pltpu.VMEM),
        ],
        out_specs=pl.BlockSpec((1, LANES, LAGS), lambda i: (i, 0, 0)),
        out_shape=jax.ShapeDtypeStruct((count, LANES, LAGS), jnp.float32),
        compiler_params=pltpu.CompilerParams(vmem_limit_bytes=32 << 20),
    )(cross, jnp.asarray(high), jnp.asarray(low))


def local(records, starts, offsets):
    axes = ("blk", "inner")
    blocks, groups = lax.axis_size("blk"), lax.axis_size("inner")
    devices = blocks * groups
    width = F // devices
    here, count = records.shape[:2]
    ids = jnp.arange(here, dtype=jnp.int32)[:, None] + REACH
    index = lax.all_gather((ids + offsets).T, "blk", axis=0)
    rows = max(width, 8)
    split = rows // width
    white = whiten(records, starts, rows)
    white = white.reshape(-1, count // split, split, 2, split, width, LANES)
    white = white.transpose(0, 4, 1, 3, 2, 5, 6).reshape(devices, -1, LANES)
    spectra = lax.all_to_all(white, axes, 0, 0, tiled=True)
    spectra = spectra.reshape(blocks, -1, 2, rows, LANES)
    cross = pair_products(spectra, index, groups)
    if split > 1:
        cross = cross.reshape(blocks, groups, 2, split, width, -1).sum(3)
    cross = lax.all_to_all(cross.reshape(devices, 2 * width, -1), axes, 0, 0, tiled=True)
    return lag_transform(cross.reshape(2 * F, -1), lag_table(width, count * groups))


def solution(mesh):
    placed = (P("blk", "inner", None), P("inner"), P("blk", None))
    return jax.shard_map(
        local, mesh=mesh, in_specs=placed, out_specs=P("inner", "blk", None), check_vma=False
    )
```

```python
import functools
import math

import jax
import jax.numpy as jnp
import numpy as np
from jax import lax
from jax.experimental import pallas as pl
from jax.experimental.pallas import tpu as pltpu
from jax.sharding import PartitionSpec as P

SEG = 1024
LAGS = 768
HALF = 32
REACH = 256
F = 512
LANES = 128
EPS = 1e-06


def bin_order():
    m = np.arange(128)
    return np.concatenate([4 * m, 4 * m + 2, 4 * m + 1, 4 * m[::-1] + 3])


def transform_tables():
    u = np.arange(256)

    def parts(bins, sign):
        angle = 2 * np.pi / SEG * (bins[:, None] * u[None, :] % SEG)
        return np.concatenate([np.cos(angle), sign * np.sin(angle)], 0).astype(np.float32)

    m = np.arange(256)
    return parts(4 * m[:128], -1), parts(4 * m[:128] + 2, -1), parts(4 * m + 1, 1)


def lag_tables(segment_count):
    bins = bin_order()[:, None]
    half = np.pi / SEG * bins * np.ones((1, LANES))
    angle = 2 * np.pi / SEG * bins * (np.arange(LAGS // 2)[None, :] + 0.5)
    factor = math.sqrt(segment_count / F) / segment_count
    tables = [np.cos(half).astype(np.float32), np.sin(half).astype(np.float32)]
    for table in (np.cos(angle) * factor, np.sin(angle) * factor):
        high = table.astype(jnp.bfloat16)
        tables += [high, (table - high.astype(np.float64)).astype(jnp.bfloat16)]
    return tables


def halves(x):
    high = x.astype(jnp.bfloat16)
    return high, (x - high.astype(jnp.float32)).astype(jnp.bfloat16)


def dot_nt(a, b, precision=None):
    return lax.dot_general(
        a, b, (((1,), (1,)), ((), ())), precision=precision, preferred_element_type=jnp.float32
    )


def dot_tn(a, b):
    return lax.dot_general(a, b, (((0,), (0,)), ((), ())), preferred_element_type=jnp.float32)


def hann_table():
    window = 0.5 - 0.5 * np.cos(2 * np.pi / SEG * np.arange(SEG))
    return np.tile(window[None, :], (8, 1)).astype(np.float32)


def whiten_kernel(
    starts_ref, records_ref, hann_ref, even0_ref, even2_ref, odd_ref, out_ref, folded_ref, band_ref, *, folds
):
    step = pl.program_id(0)
    part, count = records_ref.shape[:2]
    together, _, rows, _ = out_ref.shape[1:]
    columns = together * LANES

    @pl.when(step == 0)
    def _():
        def bins(axis):
            p = lax.broadcasted_iota(jnp.int32, (F, F), axis)
            even = jnp.where(p < 128, 4 * p, 4 * p - 510)
            return jnp.where(p < 256, even, jnp.where(p < 384, 4 * p - 1023, 2047 - 4 * p))

        distance = jnp.abs(bins(0) - bins(1))
        distance = jnp.minimum(distance, F - distance)
        band_ref[...] = jnp.where(distance <= HALF, 1.0, 0.0).astype(jnp.bfloat16)

    @pl.when(step < folds)
    def _():
        place = pl.multiple_of(step * part, part)
        samples = lax.broadcasted_iota(jnp.int32, (8, SEG), 1)
        for s in range(count):
            begin = starts_ref[s]
            window = pltpu.roll(hann_ref[...], lax.rem(begin, SEG), 1)[:1]
            early = jnp.where(samples >= begin, 1.0, 0.0)[:1] * window
            late = window - early
            x = records_ref[:, s, :SEG] * early + records_ref[:, s, SEG:] * late
            x = [x[:, 256 * j : 256 * (j + 1)] for j in range(4)]
            at = pl.ds(s * LANES + place, part)
            folded_ref[0, at, :] = (x[0] + x[2]) + (x[1] + x[3])
            folded_ref[1, at, :] = (x[0] + x[2]) - (x[1] + x[3])
            folded_ref[2, at, :] = x[0] - x[2]
            folded_ref[3, at, :] = x[1] - x[3]

    @pl.when(step >= folds)
    def _():
        at = pl.ds(pl.multiple_of((step - folds) * columns, columns), columns)
        highest = lax.Precision.HIGHEST
        s0 = dot_nt(even0_ref[...], folded_ref[0, at, :], highest)
        s2 = dot_nt(even2_ref[...], folded_ref[1, at, :], highest)
        odd = jnp.concatenate([folded_ref[2, at, :], folded_ref[3, at, :]], 0)
        s1 = dot_nt(odd_ref[...], odd, highest)
        s1_re = s1[:256, :columns] - s1[256:, columns:]
        s1_im = s1[256:, :columns] + s1[:256, columns:]
        re = jnp.concatenate([s0[:128], s2[:128], s1_re], 0)
        im = jnp.concatenate([s0[128:], s2[128:], -s1_im[:128], s1_im[128:]], 0)
        high, low = halves(re * re + im * im)
        smooth = jnp.dot(band_ref[...], high, preferred_element_type=jnp.float32)
        smooth += jnp.dot(band_ref[...], low, preferred_element_type=jnp.float32)
        scale = lax.rsqrt(smooth * (1.0 / (2 * HALF + 1)) + EPS)
        re, im = re * scale, im * scale
        for s in range(together):
            lanes = slice(s * LANES, (s + 1) * LANES)
            out_ref[:, s, 0] = re[:, lanes].reshape(-1, rows, LANES)
            out_ref[:, s, 1] = im[:, lanes].reshape(-1, rows, LANES)


def whiten(records, starts, rows):
    here, count, slot = records.shape
    part = 32
    folds = here // part
    together = 2 if count % 2 == 0 else 1
    tables = [jnp.asarray(t) for t in (hann_table(), *transform_tables())]
    return pl.pallas_call(
        functools.partial(whiten_kernel, folds=folds),
        grid=(folds + count // together,),
        in_specs=[
            pl.BlockSpec(memory_space=pltpu.SMEM),
            pl.BlockSpec((part, count, slot), lambda i: (jnp.minimum(i, folds - 1), 0, 0)),
            *[pl.BlockSpec(t.shape, lambda i: (0, 0)) for t in tables],
        ],
        out_specs=pl.BlockSpec(
            (F // rows, together, 2, rows, LANES), lambda i: (0, jnp.maximum(i - folds, 0), 0, 0, 0)
        ),
        out_shape=jax.ShapeDtypeStruct((F // rows, count, 2, rows, LANES), jnp.float32),
        scratch_shapes=[
            pltpu.VMEM((4, count * LANES, 256), jnp.float32),
            pltpu.VMEM((F, F), jnp.bfloat16),
        ],
        compiler_params=pltpu.CompilerParams(vmem_limit_bytes=56 << 20),
    )(starts, records, *tables)


def pair_kernel(index_ref, spectra_ref, out_ref, wide_ref, *, reach, turned):
    block = pl.program_id(0)
    blocks, terms, _, rows, _ = spectra_ref.shape
    pairs = index_ref.shape[1]
    groups = out_ref.shape[1]
    share = pairs // groups
    span = 2 * reach + 1

    @pl.when(block == 0)
    def _():
        def build(i, carry):
            wide_ref[i, 0], wide_ref[i, 1] = halves(spectra_ref[i].reshape(-1, LANES))
            return carry

        lax.fori_loop(0, blocks, build, 0)

    near = [lax.rem(block + (blocks - reach + j), blocks) for j in range(span)]
    left = jnp.concatenate([wide_ref[i, h] for i in near for h in range(2)], 1)
    ids = lax.broadcasted_iota(jnp.int32, (LANES, LANES), 0)

    def put(k, h, rows_here, x):
        z, q = k // share, k % share
        out_ref[0, z, h, rows_here, q * LANES : (q + 1) * LANES] = x

    def by_product(ks):
        hots = []
        for j in range(span):
            wanted = [index_ref[0, k : k + 1, :] - j * LANES for k in ks]
            hot = [jnp.where(ids == w, 1.0, 0.0).astype(jnp.bfloat16) for w in wanted]
            hot = jnp.concatenate(hot, 1)
            hots += [hot, hot]
        found = jnp.dot(left, jnp.concatenate(hots, 0), preferred_element_type=jnp.float32)
        found = found.reshape(terms, 2, rows, -1)
        for i, k in enumerate(ks):
            lanes = slice(i * LANES, (i + 1) * LANES)
            re = im = 0
            for t in range(terms):
                partner_re, partner_im = found[t, 0, :, lanes], found[t, 1, :, lanes]
                own_re, own_im = spectra_ref[block, t, 0], spectra_ref[block, t, 1]
                re = re + (own_re * partner_re + own_im * partner_im)
                im = im + (own_im * partner_re - own_re * partner_im)
            put(k, 0, slice(0, rows), re)
            put(k, 1, slice(0, rows), im)

    def by_gather(k, first):
        row = jnp.broadcast_to(index_ref[0, k : k + 1, :], (8, LANES))
        lane, part = row & (LANES - 1), lax.shift_right_logical(row, 7)
        rows_here = slice(first, first + 8)
        re = im = 0
        for t in range(terms):
            partner = []
            for h in range(2):
                found = jnp.take_along_axis(spectra_ref[near[0], t, h, rows_here], lane, axis=1)
                for j in range(1, span):
                    other = jnp.take_along_axis(spectra_ref[near[j], t, h, rows_here], lane, axis=1)
                    found = jnp.where(part == j, other, found)
                partner.append(found)
            own_re = spectra_ref[block, t, 0, rows_here]
            own_im = spectra_ref[block, t, 1, rows_here]
            re = re + (own_re * partner[0] + own_im * partner[1])
            im = im + (own_im * partner[0] - own_re * partner[1])
        put(k, 0, rows_here, re)
        put(k, 1, rows_here, im)

    chunks = [range(k, min(k + 2, pairs - turned)) for k in range(0, pairs - turned, 2)]
    gathers = [(k, first) for k in range(pairs - turned, pairs) for first in range(0, rows, 8)]
    for n, ks in enumerate(chunks):
        by_product(ks)
        for k, first in gathers[n * len(gathers) // len(chunks) : (n + 1) * len(gathers) // len(chunks)]:
            by_gather(k, first)


def pair_products(spectra, index, groups, turned=6):
    blocks, terms, _, rows, _ = spectra.shape
    pairs = index.shape[1]
    reach = -(-REACH // LANES)
    shape = (groups, 2, rows, pairs // groups * LANES)
    return pl.pallas_call(
        functools.partial(pair_kernel, reach=reach, turned=turned),
        grid=(blocks,),
        in_specs=[
            pl.BlockSpec((1, pairs, LANES), lambda b: (b, 0, 0)),
            pl.BlockSpec(memory_space=pltpu.VMEM),
        ],
        out_specs=pl.BlockSpec((1, *shape), lambda b: (b, 0, 0, 0, 0)),
        out_shape=jax.ShapeDtypeStruct((blocks, *shape), jnp.float32),
        scratch_shapes=[
            pltpu.VMEM((blocks, 2, terms * 2 * rows, LANES), jnp.bfloat16),
        ],
        compiler_params=pltpu.CompilerParams(vmem_limit_bytes=32 << 20),
    )(index, spectra)


def lag_kernel(cross_ref, turn_re_ref, turn_im_ref, even_ref, even_low_ref, odd_ref, odd_low_ref, out_ref):
    re = cross_ref[:, 0].reshape(F, LANES)
    im = cross_ref[:, 1].reshape(F, LANES)
    turn_re, turn_im = turn_re_ref[...], turn_im_ref[...]
    re, im = re * turn_re + im * turn_im, im * turn_re - re * turn_im

    def transform(x, high_ref, low_ref):
        high, low = halves(x)
        total = dot_tn(high, low_ref[...]) + dot_tn(low, high_ref[...])
        return total + dot_tn(high, high_ref[...])

    even = transform(re, even_ref, even_low_ref)
    odd = transform(im, odd_ref, odd_low_ref)
    half = LAGS // 2
    out_ref[0, :, half:] = even - odd
    before = even + odd
    mirror = LANES - 1 - lax.broadcasted_iota(jnp.int32, (LANES, LANES), 1)
    for first in range(0, half, LANES):
        turned = jnp.take_along_axis(before[:, first : first + LANES], mirror, axis=1)
        out_ref[0, :, half - first - LANES : half - first] = turned


def lag_transform(cross, tables):
    sources, _, width, columns = cross.shape
    return pl.pallas_call(
        lag_kernel,
        grid=(columns // LANES,),
        in_specs=[
            pl.BlockSpec((sources, 2, width, LANES), lambda i: (0, 0, 0, i)),
            *[pl.BlockSpec(memory_space=pltpu.VMEM) for _ in tables],
        ],
        out_specs=pl.BlockSpec((1, LANES, LAGS), lambda i: (i, 0, 0)),
        out_shape=jax.ShapeDtypeStruct((columns // LANES, LANES, LAGS), jnp.float32),
        compiler_params=pltpu.CompilerParams(vmem_limit_bytes=32 << 20),
    )(cross, *[jnp.asarray(t) for t in tables])


def local(records, starts, offsets):
    axes = ("blk", "inner")
    blocks, groups = lax.axis_size("blk"), lax.axis_size("inner")
    devices = blocks * groups
    width = F // devices
    here, count = records.shape[:2]
    ids = jnp.arange(here, dtype=jnp.int32)[:, None] + REACH
    index = lax.all_gather((ids + offsets).T, "blk", axis=0)
    rows = max(width, 8)
    split = rows // width
    white = whiten(records, starts, rows)
    white = white.reshape(-1, count // split, split, 2, split, width, LANES)
    white = white.transpose(0, 4, 1, 3, 2, 5, 6).reshape(devices, -1, LANES)
    spectra = lax.all_to_all(white, axes, 0, 0, tiled=True)
    spectra = spectra.reshape(blocks, -1, 2, rows, LANES)
    cross = pair_products(spectra, index, groups)
    if split > 1:
        cross = cross.reshape(blocks, groups, 2, split, width, -1).sum(3)
    cross = lax.all_to_all(cross.reshape(devices, 2 * width, -1), axes, 0, 0, tiled=True)
    cross = cross.reshape(devices, 2, width, -1)
    if split > 1:
        cross = cross.transpose(1, 0, 2, 3).reshape(1, 2, F, -1)
    return lag_transform(cross, lag_tables(count * groups))


def solution(mesh):
    placed = (P("blk", "inner", None), P("inner"), P("blk", None))
    return jax.shard_map(
        local, mesh=mesh, in_specs=placed, out_specs=P("inner", "blk", None), check_vma=False
    )
```

```python
import functools
import math

import jax
import jax.numpy as jnp
import numpy as np
from jax import lax
from jax.experimental import pallas as pl
from jax.experimental.pallas import tpu as pltpu
from jax.sharding import PartitionSpec as P

SEG = 1024
LAGS = 768
HALF = 32
REACH = 256
F = 512
LANES = 128
EPS = 1e-06


def bin_order():
    m = np.arange(128)
    return np.concatenate([4 * m, 4 * m + 2, 4 * m + 1, 4 * m[::-1] + 3])


def transform_tables():
    u = np.arange(256)

    def parts(bins, sign):
        angle = 2 * np.pi / SEG * (bins[:, None] * u[None, :] % SEG)
        return np.concatenate([np.cos(angle), sign * np.sin(angle)], 0).astype(np.float32)

    m = np.arange(256)
    return parts(4 * m[:128], -1), parts(4 * m[:128] + 2, -1), parts(4 * m + 1, 1)


def lag_tables(segment_count):
    bins = bin_order()[:, None]
    half = np.pi / SEG * bins * np.ones((1, LANES))
    angle = 2 * np.pi / SEG * bins * (np.arange(LAGS // 2)[None, :] + 0.5)
    factor = math.sqrt(segment_count / F) / segment_count
    tables = [np.cos(half).astype(np.float32), np.sin(half).astype(np.float32)]
    for table in (np.cos(angle) * factor, np.sin(angle) * factor):
        high = table.astype(jnp.bfloat16)
        tables += [high, (table - high.astype(np.float64)).astype(jnp.bfloat16)]
    return tables


def halves(x):
    high = x.astype(jnp.bfloat16)
    return high, (x - high.astype(jnp.float32)).astype(jnp.bfloat16)


def dot_nt(a, b, precision=None):
    return lax.dot_general(
        a, b, (((1,), (1,)), ((), ())), precision=precision, preferred_element_type=jnp.float32
    )


def dot_tn(a, b):
    return lax.dot_general(a, b, (((0,), (0,)), ((), ())), preferred_element_type=jnp.float32)


def hann_table():
    window = 0.5 - 0.5 * np.cos(2 * np.pi / SEG * np.arange(SEG))
    return np.tile(window[None, :], (8, 1)).astype(np.float32)


def whiten_kernel(
    starts_ref, records_hbm, hann_hbm, even0_hbm, even2_hbm, odd_hbm, out_hbm,
    records_ref, hann_ref, even0_ref, even2_ref, odd_ref, folded_ref, band_ref, out_ref,
    table_sems, record_sems, out_sems,
):
    here, count = records_ref.shape[:2]
    rows = out_ref.shape[4]
    parts, halves_out = record_sems.shape[0], out_sems.shape[0]
    part, together = here // parts, count // halves_out
    columns = together * LANES

    tables = [(hann_hbm, hann_ref), (even0_hbm, even0_ref), (even2_hbm, even2_ref), (odd_hbm, odd_ref)]
    tables = [pltpu.make_async_copy(s, d, table_sems.at[i]) for i, (s, d) in enumerate(tables)]
    pieces = [pl.ds(p * part, part) for p in range(parts)]
    pieces = [
        pltpu.make_async_copy(records_hbm.at[at], records_ref.at[at], record_sems.at[p])
        for p, at in enumerate(pieces)
    ]
    for copy in [tables[0], *pieces, *tables[1:]]:
        copy.start()

    def bins(axis):
        p = lax.broadcasted_iota(jnp.int32, (F, F), axis)
        even = jnp.where(p < 128, 4 * p, 4 * p - 510)
        return jnp.where(p < 256, even, jnp.where(p < 384, 4 * p - 1023, 2047 - 4 * p))

    distance = jnp.abs(bins(0) - bins(1))
    distance = jnp.minimum(distance, F - distance)
    band_ref[...] = jnp.where(distance <= HALF, 1.0, 0.0).astype(jnp.bfloat16)

    samples = lax.broadcasted_iota(jnp.int32, (8, SEG), 1)
    tables[0].wait()
    windows = []
    for s in range(count):
        begin = starts_ref[s]
        window = pltpu.roll(hann_ref[...], lax.rem(begin, SEG), 1)[:1]
        early = jnp.where(samples >= begin, 1.0, 0.0)[:1] * window
        windows.append((early, window - early))
    for p, copy in enumerate(pieces):
        copy.wait()
        for s, (early, late) in enumerate(windows):
            at = slice(p * part, (p + 1) * part)
            x = records_ref[at, s, :SEG] * early + records_ref[at, s, SEG:] * late
            x = [x[:, 256 * j : 256 * (j + 1)] for j in range(4)]
            at = slice(s * LANES + p * part, s * LANES + (p + 1) * part)
            folded_ref[0, at, :] = (x[0] + x[2]) + (x[1] + x[3])
            folded_ref[1, at, :] = (x[0] + x[2]) - (x[1] + x[3])
            folded_ref[2, at, :] = x[0] - x[2]
            folded_ref[3, at, :] = x[1] - x[3]

    for copy in tables[1:]:
        copy.wait()
    highest = lax.Precision.HIGHEST
    done = []
    for n in range(halves_out):
        at = slice(n * columns, (n + 1) * columns)
        s0 = dot_nt(even0_ref[...], folded_ref[0, at, :], highest)
        s2 = dot_nt(even2_ref[...], folded_ref[1, at, :], highest)
        odd = jnp.concatenate([folded_ref[2, at, :], folded_ref[3, at, :]], 0)
        s1 = dot_nt(odd_ref[...], odd, highest)
        s1_re = s1[:256, :columns] - s1[256:, columns:]
        s1_im = s1[256:, :columns] + s1[:256, columns:]
        re = jnp.concatenate([s0[:128], s2[:128], s1_re], 0)
        im = jnp.concatenate([s0[128:], s2[128:], -s1_im[:128], s1_im[128:]], 0)
        high, low = halves(re * re + im * im)
        smooth = jnp.dot(band_ref[...], high, preferred_element_type=jnp.float32)
        smooth += jnp.dot(band_ref[...], low, preferred_element_type=jnp.float32)
        scale = lax.rsqrt(smooth * (1.0 / (2 * HALF + 1)) + EPS)
        re, im = re * scale, im * scale
        for s in range(together):
            lanes = slice(s * LANES, (s + 1) * LANES)
            out_ref[n, :, s, 0] = re[:, lanes].reshape(-1, rows, LANES)
            out_ref[n, :, s, 1] = im[:, lanes].reshape(-1, rows, LANES)
        segments = pl.ds(n * together, together)
        done.append(pltpu.make_async_copy(out_ref.at[n], out_hbm.at[:, segments], out_sems.at[n]))
        done[n].start()
    for copy in done:
        copy.wait()


def whiten(records, starts, rows):
    count = records.shape[1]
    parts = 4
    splits = 2 if count % 2 == 0 else 1
    tables = [jnp.asarray(t) for t in (hann_table(), *transform_tables())]
    return pl.pallas_call(
        whiten_kernel,
        in_specs=[
            pl.BlockSpec(memory_space=pltpu.SMEM),
            *[pl.BlockSpec(memory_space=pl.ANY) for _ in range(1 + len(tables))],
        ],
        out_specs=pl.BlockSpec(memory_space=pl.ANY),
        out_shape=jax.ShapeDtypeStruct((F // rows, count, 2, rows, LANES), jnp.float32),
        scratch_shapes=[
            pltpu.VMEM(records.shape, jnp.float32),
            *[pltpu.VMEM(t.shape, jnp.float32) for t in tables],
            pltpu.VMEM((4, count * LANES, 256), jnp.float32),
            pltpu.VMEM((F, F), jnp.bfloat16),
            pltpu.VMEM((splits, F // rows, count // splits, 2, rows, LANES), jnp.float32),
            pltpu.SemaphoreType.DMA((len(tables),)),
            pltpu.SemaphoreType.DMA((parts,)),
            pltpu.SemaphoreType.DMA((splits,)),
        ],
        compiler_params=pltpu.CompilerParams(vmem_limit_bytes=56 << 20),
    )(starts, records, *tables)


def pair_kernel(index_ref, spectra_ref, out_ref, wide_ref, *, reach, turned):
    blocks, terms, _, rows, _ = spectra_ref.shape

    def build(i, carry):
        wide_ref[i, 0], wide_ref[i, 1] = halves(spectra_ref[i].reshape(-1, LANES))
        return carry

    lax.fori_loop(0, blocks, build, 0)
    ids = lax.broadcasted_iota(jnp.int32, (LANES, LANES), 0)

    def one_block(block, carry):
        pair_block(block, index_ref, spectra_ref, out_ref, wide_ref, ids, reach, turned)
        return carry

    lax.fori_loop(0, blocks, one_block, 0)


def pair_block(block, index_ref, spectra_ref, out_ref, wide_ref, ids, reach, turned):
    blocks, terms, _, rows, _ = spectra_ref.shape
    pairs = index_ref.shape[1]
    groups = out_ref.shape[1]
    share = pairs // groups
    span = 2 * reach + 1
    near = [lax.rem(block + (blocks - reach + j), blocks) for j in range(span)]
    left = jnp.concatenate([wide_ref[i, h] for i in near for h in range(2)], 1)

    def put(k, h, rows_here, x):
        z, q = k // share, k % share
        out_ref[block, z, h, rows_here, q * LANES : (q + 1) * LANES] = x

    def by_product(ks):
        hots = []
        for j in range(span):
            wanted = [index_ref[block, k : k + 1, :] - j * LANES for k in ks]
            hot = [jnp.where(ids == w, 1.0, 0.0).astype(jnp.bfloat16) for w in wanted]
            hot = jnp.concatenate(hot, 1)
            hots += [hot, hot]
        found = jnp.dot(left, jnp.concatenate(hots, 0), preferred_element_type=jnp.float32)
        found = found.reshape(terms, 2, rows, -1)
        for i, k in enumerate(ks):
            lanes = slice(i * LANES, (i + 1) * LANES)
            re = im = 0
            for t in range(terms):
                partner_re, partner_im = found[t, 0, :, lanes], found[t, 1, :, lanes]
                own_re, own_im = spectra_ref[block, t, 0], spectra_ref[block, t, 1]
                re = re + (own_re * partner_re + own_im * partner_im)
                im = im + (own_im * partner_re - own_re * partner_im)
            put(k, 0, slice(0, rows), re)
            put(k, 1, slice(0, rows), im)

    def by_gather(k, first):
        row = jnp.broadcast_to(index_ref[block, k : k + 1, :], (8, LANES))
        lane, part = row & (LANES - 1), lax.shift_right_logical(row, 7)
        rows_here = slice(first, first + 8)
        re = im = 0
        for t in range(terms):
            partner = []
            for h in range(2):
                found = jnp.take_along_axis(spectra_ref[near[0], t, h, rows_here], lane, axis=1)
                for j in range(1, span):
                    other = jnp.take_along_axis(spectra_ref[near[j], t, h, rows_here], lane, axis=1)
                    found = jnp.where(part == j, other, found)
                partner.append(found)
            own_re = spectra_ref[block, t, 0, rows_here]
            own_im = spectra_ref[block, t, 1, rows_here]
            re = re + (own_re * partner[0] + own_im * partner[1])
            im = im + (own_im * partner[0] - own_re * partner[1])
        put(k, 0, rows_here, re)
        put(k, 1, rows_here, im)

    chunks = [range(k, min(k + 2, pairs - turned)) for k in range(0, pairs - turned, 2)]
    gathers = [(k, first) for k in range(pairs - turned, pairs) for first in range(0, rows, 8)]
    for n, ks in enumerate(chunks):
        by_product(ks)
        for k, first in gathers[n * len(gathers) // len(chunks) : (n + 1) * len(gathers) // len(chunks)]:
            by_gather(k, first)


def pair_products(spectra, index, groups, turned=6):
    blocks, terms, _, rows, _ = spectra.shape
    pairs = index.shape[1]
    reach = -(-REACH // LANES)
    shape = (groups, 2, rows, pairs // groups * LANES)
    return pl.pallas_call(
        functools.partial(pair_kernel, reach=reach, turned=turned),
        in_specs=[pl.BlockSpec(memory_space=pltpu.VMEM)] * 2,
        out_specs=pl.BlockSpec(memory_space=pltpu.VMEM),
        out_shape=jax.ShapeDtypeStruct((blocks, *shape), jnp.float32),
        scratch_shapes=[
            pltpu.VMEM((blocks, 2, terms * 2 * rows, LANES), jnp.bfloat16),
        ],
        compiler_params=pltpu.CompilerParams(vmem_limit_bytes=32 << 20),
    )(index, spectra)


def lag_kernel(cross_ref, turn_re_ref, turn_im_ref, even_ref, even_low_ref, odd_ref, odd_low_ref, out_hbm, out_ref, sems):
    turn_re, turn_im = turn_re_ref[...], turn_im_ref[...]
    half = LAGS // 2
    mirror = LANES - 1 - lax.broadcasted_iota(jnp.int32, (LANES, LANES), 1)

    def transform(x, high_ref, low_ref):
        high, low = halves(x)
        total = dot_tn(high, low_ref[...]) + dot_tn(low, high_ref[...])
        return total + dot_tn(high, high_ref[...])

    done = []
    for i in range(out_ref.shape[0]):
        lanes = slice(i * LANES, (i + 1) * LANES)
        re = cross_ref[:, 0, :, lanes].reshape(F, LANES)
        im = cross_ref[:, 1, :, lanes].reshape(F, LANES)
        re, im = re * turn_re + im * turn_im, im * turn_re - re * turn_im
        even = transform(re, even_ref, even_low_ref)
        odd = transform(im, odd_ref, odd_low_ref)
        out_ref[i, :, half:] = even - odd
        before = even + odd
        for first in range(0, half, LANES):
            turned = jnp.take_along_axis(before[:, first : first + LANES], mirror, axis=1)
            out_ref[i, :, half - first - LANES : half - first] = turned
        done.append(pltpu.make_async_copy(out_ref.at[i], out_hbm.at[i], sems.at[i]))
        done[i].start()
    for copy in done:
        copy.wait()


def lag_transform(cross, tables):
    count = cross.shape[3] // LANES
    return pl.pallas_call(
        lag_kernel,
        in_specs=[pl.BlockSpec(memory_space=pltpu.VMEM)] * (1 + len(tables)),
        out_specs=pl.BlockSpec(memory_space=pl.ANY),
        out_shape=jax.ShapeDtypeStruct((count, LANES, LAGS), jnp.float32),
        scratch_shapes=[
            pltpu.VMEM((count, LANES, LAGS), jnp.float32),
            pltpu.SemaphoreType.DMA((count,)),
        ],
        compiler_params=pltpu.CompilerParams(vmem_limit_bytes=32 << 20),
    )(cross, *[jnp.asarray(t) for t in tables])


def local(records, starts, offsets):
    axes = ("blk", "inner")
    blocks, groups = lax.axis_size("blk"), lax.axis_size("inner")
    devices = blocks * groups
    width = F // devices
    here, count = records.shape[:2]
    ids = jnp.arange(here, dtype=jnp.int32)[:, None] + REACH
    index = lax.all_gather((ids + offsets).T, "blk", axis=0)
    rows = max(width, 8)
    split = rows // width
    white = whiten(records, starts, rows)
    white = white.reshape(-1, count // split, split, 2, split, width, LANES)
    white = white.transpose(0, 4, 1, 3, 2, 5, 6).reshape(devices, -1, LANES)
    spectra = lax.all_to_all(white, axes, 0, 0, tiled=True)
    spectra = spectra.reshape(blocks, -1, 2, rows, LANES)
    cross = pair_products(spectra, index, groups)
    if split > 1:
        cross = cross.reshape(blocks, groups, 2, split, width, -1).sum(3)
    cross = lax.all_to_all(cross.reshape(devices, 2 * width, -1), axes, 0, 0, tiled=True)
    cross = cross.reshape(devices, 2, width, -1)
    if split > 1:
        cross = cross.transpose(1, 0, 2, 3).reshape(1, 2, F, -1)
    return lag_transform(cross, lag_tables(count * groups))


def solution(mesh):
    placed = (P("blk", "inner", None), P("inner"), P("blk", None))
    return jax.shard_map(
        local, mesh=mesh, in_specs=placed, out_specs=P("inner", "blk", None), check_vma=False
    )
```

```python
import functools
import math

import jax
import jax.numpy as jnp
import numpy as np
from jax import lax
from jax.experimental import pallas as pl
from jax.experimental.pallas import tpu as pltpu
from jax.sharding import PartitionSpec as P

SEG = 1024
LAGS = 768
HALF = 32
REACH = 256
F = 512
LANES = 128
EPS = 1e-06


def bin_order():
    m = np.arange(128)
    return np.concatenate([4 * m, 4 * m + 2, 4 * m + 1, 4 * m[::-1] + 3])


def transform_tables():
    u = np.arange(256)

    def parts(bins, sign):
        angle = 2 * np.pi / SEG * (bins[:, None] * u[None, :] % SEG)
        return np.concatenate([np.cos(angle), sign * np.sin(angle)], 0).astype(np.float32)

    m = np.arange(256)
    return parts(4 * m[:128], -1), parts(4 * m[:128] + 2, -1), parts(4 * m + 1, 1)


def lag_tables(segment_count):
    bins = bin_order()[:, None]
    half = np.pi / SEG * bins * np.ones((1, LANES))
    angle = 2 * np.pi / SEG * bins * (np.arange(LAGS // 2)[None, :] + 0.5)
    factor = math.sqrt(segment_count / F) / segment_count
    tables = [np.cos(half).astype(np.float32), np.sin(half).astype(np.float32)]
    for table in (np.cos(angle) * factor, np.sin(angle) * factor):
        high = table.astype(jnp.bfloat16)
        tables += [high, (table - high.astype(np.float64)).astype(jnp.bfloat16)]
    return tables


def halves(x):
    high = x.astype(jnp.bfloat16)
    return high, (x - high.astype(jnp.float32)).astype(jnp.bfloat16)


def dot_nt(a, b, precision=None):
    return lax.dot_general(
        a, b, (((1,), (1,)), ((), ())), precision=precision, preferred_element_type=jnp.float32
    )


def dot_tn(a, b):
    return lax.dot_general(a, b, (((0,), (0,)), ((), ())), preferred_element_type=jnp.float32)


def hann_table():
    window = 0.5 - 0.5 * np.cos(2 * np.pi / SEG * np.arange(SEG))
    return np.tile(window[None, :], (8, 1)).astype(np.float32)


def whiten_kernel(
    starts_ref, records_hbm, hann_hbm, even0_hbm, even2_hbm, odd_hbm, *rest
):
    *outs_hbm, records_ref, hann_ref, even0_ref, even2_ref, odd_ref, folded_ref, band_ref = rest[:-4]
    out_ref, table_sems, record_sems, out_sems = rest[-4:]
    here, count = records_ref.shape[:2]
    rows = out_ref.shape[5]
    parts, (halves_out, chunks) = record_sems.shape[0], out_sems.shape
    part, together = here // parts, count // halves_out
    columns = together * LANES

    tables = [(hann_hbm, hann_ref), (even0_hbm, even0_ref), (even2_hbm, even2_ref), (odd_hbm, odd_ref)]
    tables = [pltpu.make_async_copy(s, d, table_sems.at[i]) for i, (s, d) in enumerate(tables)]
    pieces = [pl.ds(p * part, part) for p in range(parts)]
    pieces = [
        pltpu.make_async_copy(records_hbm.at[at], records_ref.at[at], record_sems.at[p])
        for p, at in enumerate(pieces)
    ]
    for copy in [tables[0], *pieces, *tables[1:]]:
        copy.start()

    def bins(axis):
        p = lax.broadcasted_iota(jnp.int32, (F, F), axis)
        even = jnp.where(p < 128, 4 * p, 4 * p - 510)
        return jnp.where(p < 256, even, jnp.where(p < 384, 4 * p - 1023, 2047 - 4 * p))

    distance = jnp.abs(bins(0) - bins(1))
    distance = jnp.minimum(distance, F - distance)
    band_ref[...] = jnp.where(distance <= HALF, 1.0, 0.0).astype(jnp.bfloat16)

    samples = lax.broadcasted_iota(jnp.int32, (8, SEG), 1)
    tables[0].wait()
    windows = []
    for s in range(count):
        begin = starts_ref[s]
        window = pltpu.roll(hann_ref[...], lax.rem(begin, SEG), 1)[:1]
        early = jnp.where(samples >= begin, 1.0, 0.0)[:1] * window
        windows.append((early, window - early))
    for p, copy in enumerate(pieces):
        copy.wait()
        for s, (early, late) in enumerate(windows):
            at = slice(p * part, (p + 1) * part)
            x = records_ref[at, s, :SEG] * early + records_ref[at, s, SEG:] * late
            x = [x[:, 256 * j : 256 * (j + 1)] for j in range(4)]
            at = slice(s * LANES + p * part, s * LANES + (p + 1) * part)
            folded_ref[0, at, :] = (x[0] + x[2]) + (x[1] + x[3])
            folded_ref[1, at, :] = (x[0] + x[2]) - (x[1] + x[3])
            folded_ref[2, at, :] = x[0] - x[2]
            folded_ref[3, at, :] = x[1] - x[3]

    for copy in tables[1:]:
        copy.wait()
    highest = lax.Precision.HIGHEST
    done = []
    for n in range(halves_out):
        at = slice(n * columns, (n + 1) * columns)
        s0 = dot_nt(even0_ref[...], folded_ref[0, at, :], highest)
        s2 = dot_nt(even2_ref[...], folded_ref[1, at, :], highest)
        odd = jnp.concatenate([folded_ref[2, at, :], folded_ref[3, at, :]], 0)
        s1 = dot_nt(odd_ref[...], odd, highest)
        s1_re = s1[:256, :columns] - s1[256:, columns:]
        s1_im = s1[256:, :columns] + s1[:256, columns:]
        re = jnp.concatenate([s0[:128], s2[:128], s1_re], 0)
        im = jnp.concatenate([s0[128:], s2[128:], -s1_im[:128], s1_im[128:]], 0)
        high, low = halves(re * re + im * im)
        smooth = jnp.dot(band_ref[...], high, preferred_element_type=jnp.float32)
        smooth += jnp.dot(band_ref[...], low, preferred_element_type=jnp.float32)
        scale = lax.rsqrt(smooth * (1.0 / (2 * HALF + 1)) + EPS)
        re, im = re * scale, im * scale
        segments = pl.ds(n * together, together)
        for c, out_hbm in enumerate(outs_hbm):
            mine = slice(c * F // chunks, (c + 1) * F // chunks)
            for s in range(together):
                lanes = slice(s * LANES, (s + 1) * LANES)
                out_ref[n, c, :, s, 0] = re[mine, lanes].reshape(-1, rows, LANES)
                out_ref[n, c, :, s, 1] = im[mine, lanes].reshape(-1, rows, LANES)
            copy = pltpu.make_async_copy(out_ref.at[n, c], out_hbm.at[:, segments], out_sems.at[n, c])
            copy.start()
            done.append(copy)
    for copy in done:
        copy.wait()


def whiten(records, starts, rows, chunks):
    count = records.shape[1]
    parts = 4
    splits = 2 if count % 2 == 0 else 1
    per_chunk = F // chunks // rows
    tables = [jnp.asarray(t) for t in (hann_table(), *transform_tables())]
    return pl.pallas_call(
        whiten_kernel,
        in_specs=[
            pl.BlockSpec(memory_space=pltpu.SMEM),
            *[pl.BlockSpec(memory_space=pl.ANY) for _ in range(1 + len(tables))],
        ],
        out_specs=[pl.BlockSpec(memory_space=pl.ANY)] * chunks,
        out_shape=[jax.ShapeDtypeStruct((per_chunk, count, 2, rows, LANES), jnp.float32)] * chunks,
        scratch_shapes=[
            pltpu.VMEM(records.shape, jnp.float32),
            *[pltpu.VMEM(t.shape, jnp.float32) for t in tables],
            pltpu.VMEM((4, count * LANES, 256), jnp.float32),
            pltpu.VMEM((F, F), jnp.bfloat16),
            pltpu.VMEM((splits, chunks, per_chunk, count // splits, 2, rows, LANES), jnp.float32),
            pltpu.SemaphoreType.DMA((len(tables),)),
            pltpu.SemaphoreType.DMA((parts,)),
            pltpu.SemaphoreType.DMA((splits, chunks)),
        ],
        compiler_params=pltpu.CompilerParams(vmem_limit_bytes=56 << 20),
    )(starts, records, *tables)


def pair_kernel(index_ref, spectra_ref, out_ref, wide_ref, *, reach, turned):
    blocks, terms, _, rows, _ = spectra_ref.shape

    def build(i, carry):
        wide_ref[i, 0], wide_ref[i, 1] = halves(spectra_ref[i].reshape(-1, LANES))
        return carry

    lax.fori_loop(0, blocks, build, 0)
    ids = lax.broadcasted_iota(jnp.int32, (LANES, LANES), 0)

    def one_block(block, carry):
        pair_block(block, index_ref, spectra_ref, out_ref, wide_ref, ids, reach, turned)
        return carry

    lax.fori_loop(0, blocks, one_block, 0)


def pair_block(block, index_ref, spectra_ref, out_ref, wide_ref, ids, reach, turned):
    blocks, terms, _, rows, _ = spectra_ref.shape
    pairs = index_ref.shape[1]
    groups = out_ref.shape[1]
    share = pairs // groups
    span = 2 * reach + 1
    near = [lax.rem(block + (blocks - reach + j), blocks) for j in range(span)]
    left = jnp.concatenate([wide_ref[i, h] for i in near for h in range(2)], 1)

    def put(k, h, rows_here, x):
        z, q = k // share, k % share
        out_ref[block, z, h, rows_here, q * LANES : (q + 1) * LANES] = x

    def by_product(ks):
        hots = []
        for j in range(span):
            wanted = [index_ref[block, k : k + 1, :] - j * LANES for k in ks]
            hot = [jnp.where(ids == w, 1.0, 0.0).astype(jnp.bfloat16) for w in wanted]
            hot = jnp.concatenate(hot, 1)
            hots += [hot, hot]
        found = jnp.dot(left, jnp.concatenate(hots, 0), preferred_element_type=jnp.float32)
        found = found.reshape(terms, 2, rows, -1)
        for i, k in enumerate(ks):
            lanes = slice(i * LANES, (i + 1) * LANES)
            re = im = 0
            for t in range(terms):
                partner_re, partner_im = found[t, 0, :, lanes], found[t, 1, :, lanes]
                own_re, own_im = spectra_ref[block, t, 0], spectra_ref[block, t, 1]
                re = re + (own_re * partner_re + own_im * partner_im)
                im = im + (own_im * partner_re - own_re * partner_im)
            put(k, 0, slice(0, rows), re)
            put(k, 1, slice(0, rows), im)

    def by_gather(k, first):
        row = jnp.broadcast_to(index_ref[block, k : k + 1, :], (8, LANES))
        lane, part = row & (LANES - 1), lax.shift_right_logical(row, 7)
        rows_here = slice(first, first + 8)
        re = im = 0
        for t in range(terms):
            partner = []
            for h in range(2):
                found = jnp.take_along_axis(spectra_ref[near[0], t, h, rows_here], lane, axis=1)
                for j in range(1, span):
                    other = jnp.take_along_axis(spectra_ref[near[j], t, h, rows_here], lane, axis=1)
                    found = jnp.where(part == j, other, found)
                partner.append(found)
            own_re = spectra_ref[block, t, 0, rows_here]
            own_im = spectra_ref[block, t, 1, rows_here]
            re = re + (own_re * partner[0] + own_im * partner[1])
            im = im + (own_im * partner[0] - own_re * partner[1])
        put(k, 0, rows_here, re)
        put(k, 1, rows_here, im)

    chunks = [range(k, min(k + 2, pairs - turned)) for k in range(0, pairs - turned, 2)]
    gathers = [(k, first) for k in range(pairs - turned, pairs) for first in range(0, rows, 8)]
    for n, ks in enumerate(chunks):
        by_product(ks)
        for k, first in gathers[n * len(gathers) // len(chunks) : (n + 1) * len(gathers) // len(chunks)]:
            by_gather(k, first)


def pair_products(spectra, index, groups, turned=6):
    blocks, terms, _, rows, _ = spectra.shape
    pairs = index.shape[1]
    reach = -(-REACH // LANES)
    shape = (groups, 2, rows, pairs // groups * LANES)
    return pl.pallas_call(
        functools.partial(pair_kernel, reach=reach, turned=turned),
        in_specs=[pl.BlockSpec(memory_space=pltpu.VMEM)] * 2,
        out_specs=pl.BlockSpec(memory_space=pltpu.VMEM),
        out_shape=jax.ShapeDtypeStruct((blocks, *shape), jnp.float32),
        scratch_shapes=[
            pltpu.VMEM((blocks, 2, terms * 2 * rows, LANES), jnp.bfloat16),
        ],
        compiler_params=pltpu.CompilerParams(vmem_limit_bytes=10 << 20),
        cost_estimate=pl.CostEstimate(
            flops=8 * (2 * reach + 1) * LANES * pairs * LANES * spectra.size // LANES,
            bytes_accessed=8 * spectra.size,
            transcendentals=0,
        ),
    )(index, spectra)


def lag_kernel(cross_ref, turn_re_ref, turn_im_ref, even_ref, even_low_ref, odd_ref, odd_low_ref, *rest):
    earlier_ref = rest[0] if len(rest) == 4 else None
    last = len(rest) > 1
    out_ref = rest[-2] if last else rest[0]
    bins = cross_ref.shape[0] * cross_ref.shape[2]
    turn_re, turn_im = turn_re_ref[...], turn_im_ref[...]
    half = LAGS // 2
    mirror = LANES - 1 - lax.broadcasted_iota(jnp.int32, (LANES, LANES), 1)

    def transform(x, high_ref, low_ref):
        high, low = halves(x)
        total = dot_tn(high, low_ref[...]) + dot_tn(low, high_ref[...])
        return total + dot_tn(high, high_ref[...])

    done = []
    for i in range(out_ref.shape[0]):
        lanes = slice(i * LANES, (i + 1) * LANES)
        re = cross_ref[:, 0, :, lanes].reshape(bins, LANES)
        im = cross_ref[:, 1, :, lanes].reshape(bins, LANES)
        re, im = re * turn_re + im * turn_im, im * turn_re - re * turn_im
        even = transform(re, even_ref, even_low_ref)
        odd = transform(im, odd_ref, odd_low_ref)
        pieces = [(half, even - odd)]
        before = even + odd
        for first in range(0, half, LANES):
            turned = jnp.take_along_axis(before[:, first : first + LANES], mirror, axis=1)
            pieces.append((half - first - LANES, turned))
        for first, x in pieces:
            at = slice(first, first + x.shape[1])
            out_ref[i, :, at] = x if earlier_ref is None else x + earlier_ref[i, :, at]
        if last:
            done.append(pltpu.make_async_copy(out_ref.at[i], rest[-3].at[i], rest[-1].at[i]))
            done[i].start()
    for copy in done:
        copy.wait()


def lag_transform(cross, tables, earlier, last):
    count = cross.shape[3] // LANES
    given = [cross, *[jnp.asarray(t) for t in tables]]
    if earlier is not None:
        given.append(earlier)
    shape = (count, LANES, LAGS)
    return pl.pallas_call(
        lag_kernel,
        in_specs=[pl.BlockSpec(memory_space=pltpu.VMEM)] * len(given),
        out_specs=pl.BlockSpec(memory_space=pl.ANY if last else pltpu.VMEM),
        out_shape=jax.ShapeDtypeStruct(shape, jnp.float32),
        scratch_shapes=[pltpu.VMEM(shape, jnp.float32), pltpu.SemaphoreType.DMA((count,))] if last else [],
        compiler_params=pltpu.CompilerParams(vmem_limit_bytes=10 << 20),
        cost_estimate=pl.CostEstimate(
            flops=6 * LAGS * cross.size, bytes_accessed=8 * cross.size, transcendentals=0
        ),
    )(*given)


def local(records, starts, offsets):
    axes = ("blk", "inner")
    blocks, groups = lax.axis_size("blk"), lax.axis_size("inner")
    devices = blocks * groups
    here, count = records.shape[:2]
    ids = jnp.arange(here, dtype=jnp.int32)[:, None] + REACH
    index = lax.all_gather((ids + offsets).T, "blk", axis=0)
    chunks = 2 if F // devices % 16 == 0 else 1
    width = F // devices // chunks
    rows = max(width, 8)
    split = rows // width
    tables = lag_tables(count * groups)
    lags = None
    spectra = []
    for white in whiten(records, starts, rows, chunks):
        white = white.reshape(-1, count // split, split, 2, split, width, LANES)
        white = white.transpose(0, 4, 1, 3, 2, 5, 6).reshape(devices, -1, LANES)
        white = lax.all_to_all(white, axes, 0, 0, tiled=True)
        spectra.append(white.reshape(blocks, -1, 2, rows, LANES))
    for c in range(chunks):
        cross = pair_products(spectra[c], index, groups)
        if split > 1:
            cross = cross.reshape(blocks, groups, 2, split, width, -1).sum(3)
        cross = lax.all_to_all(cross.reshape(devices, 2 * width, -1), axes, 0, 0, tiled=True)
        cross = cross.reshape(devices, 2, width, -1)
        if split > 1:
            cross = cross.transpose(1, 0, 2, 3).reshape(1, 2, F // chunks, -1)
        mine = [t[c * F // chunks : (c + 1) * F // chunks] for t in tables]
        lags = lag_transform(cross, mine, lags, c == chunks - 1)
    return lags


def solution(mesh):
    placed = (P("blk", "inner", None), P("inner"), P("blk", None))
    return jax.shard_map(
        local, mesh=mesh, in_specs=placed, out_specs=P("inner", "blk", None), check_vma=False
    )
```

```python
import functools
import math

import jax
import jax.numpy as jnp
import numpy as np
from jax import lax
from jax.experimental import pallas as pl
from jax.experimental.pallas import tpu as pltpu
from jax.sharding import PartitionSpec as P

SEG = 1024
LAGS = 768
HALF = 32
REACH = 256
F = 512
LANES = 128
EPS = 1e-06


def bin_order():
    m = np.arange(128)
    return np.concatenate([4 * m, 4 * m + 2, 4 * m + 1, 4 * m[::-1] + 3])


def transform_tables():
    u = np.arange(256)

    def parts(bins, sign):
        angle = 2 * np.pi / SEG * (bins[:, None] * u[None, :] % SEG)
        return np.concatenate([np.cos(angle), sign * np.sin(angle)], 0).astype(np.float32)

    m = np.arange(256)
    return parts(4 * m[:128], -1), parts(4 * m[:128] + 2, -1), parts(4 * m + 1, 1)


def lag_tables(segment_count):
    bins = bin_order()[:, None]
    angle = 2 * np.pi / SEG * bins * (np.arange(LAGS // 2)[None, :] + 0.5)
    factor = math.sqrt(segment_count / F) / segment_count
    tables = []
    for table in (np.cos(angle) * factor, np.sin(angle) * factor):
        high = table.astype(jnp.bfloat16)
        tables += [high, (table - high.astype(np.float64)).astype(jnp.bfloat16)]
    return np.stack(tables)


def turn_table(devices, width, rows, chunks):
    half = np.pi / SEG * bin_order().reshape(chunks, devices, 1, 1, width, 1)
    half = np.broadcast_to(half, (chunks, devices, 1, rows // width, width, 1))
    table = np.concatenate([np.cos(half), np.sin(half)], 2)
    return jnp.asarray(table.reshape(chunks, devices, 2, rows, 1).astype(np.float32))


def halves(x):
    high = x.astype(jnp.bfloat16)
    return high, (x - high.astype(jnp.float32)).astype(jnp.bfloat16)


def dot_nt(a, b, precision=None):
    return lax.dot_general(
        a, b, (((1,), (1,)), ((), ())), precision=precision, preferred_element_type=jnp.float32
    )


def dot_tn(a, b):
    return lax.dot_general(a, b, (((0,), (0,)), ((), ())), preferred_element_type=jnp.float32)


def hann_table():
    window = 0.5 - 0.5 * np.cos(2 * np.pi / SEG * np.arange(SEG))
    return np.tile(window[None, :], (8, 1)).astype(np.float32)


def whiten_kernel(
    starts_ref, records_hbm, hann_hbm, even0_hbm, even2_hbm, odd_hbm, *rest
):
    *outs_hbm, records_ref, hann_ref, even0_ref, even2_ref, odd_ref, folded_ref, band_ref = rest[:-4]
    out_ref, table_sems, record_sems, out_sems = rest[-4:]
    here, count = records_ref.shape[:2]
    rows = out_ref.shape[5]
    parts, (halves_out, chunks) = record_sems.shape[0], out_sems.shape
    part, together = here // parts, count // halves_out
    columns = together * LANES

    tables = [(hann_hbm, hann_ref), (even0_hbm, even0_ref), (even2_hbm, even2_ref), (odd_hbm, odd_ref)]
    tables = [pltpu.make_async_copy(s, d, table_sems.at[i]) for i, (s, d) in enumerate(tables)]
    pieces = [pl.ds(p * part, part) for p in range(parts)]
    pieces = [
        pltpu.make_async_copy(records_hbm.at[at], records_ref.at[at], record_sems.at[p])
        for p, at in enumerate(pieces)
    ]
    for copy in [tables[0], *pieces, *tables[1:]]:
        copy.start()

    def bins(axis):
        p = lax.broadcasted_iota(jnp.int32, (F, F), axis)
        even = jnp.where(p < 128, 4 * p, 4 * p - 510)
        return jnp.where(p < 256, even, jnp.where(p < 384, 4 * p - 1023, 2047 - 4 * p))

    distance = jnp.abs(bins(0) - bins(1))
    distance = jnp.minimum(distance, F - distance)
    band_ref[...] = jnp.where(distance <= HALF, 1.0, 0.0).astype(jnp.bfloat16)

    samples = lax.broadcasted_iota(jnp.int32, (8, SEG), 1)
    tables[0].wait()
    windows = []
    for s in range(count):
        begin = starts_ref[s]
        window = pltpu.roll(hann_ref[...], lax.rem(begin, SEG), 1)[:1]
        early = jnp.where(samples >= begin, 1.0, 0.0)[:1] * window
        windows.append((early, window - early))
    for p, copy in enumerate(pieces):
        copy.wait()
        for s, (early, late) in enumerate(windows):
            at = slice(p * part, (p + 1) * part)
            x = records_ref[at, s, :SEG] * early + records_ref[at, s, SEG:] * late
            x = [x[:, 256 * j : 256 * (j + 1)] for j in range(4)]
            at = slice(s * LANES + p * part, s * LANES + (p + 1) * part)
            folded_ref[0, at, :] = (x[0] + x[2]) + (x[1] + x[3])
            folded_ref[1, at, :] = (x[0] + x[2]) - (x[1] + x[3])
            folded_ref[2, at, :] = x[0] - x[2]
            folded_ref[3, at, :] = x[1] - x[3]

    for copy in tables[1:]:
        copy.wait()
    highest = lax.Precision.HIGHEST
    done = []
    for n in range(halves_out):
        at = slice(n * columns, (n + 1) * columns)
        s0 = dot_nt(even0_ref[...], folded_ref[0, at, :], highest)
        s2 = dot_nt(even2_ref[...], folded_ref[1, at, :], highest)
        odd = jnp.concatenate([folded_ref[2, at, :], folded_ref[3, at, :]], 0)
        s1 = dot_nt(odd_ref[...], odd, highest)
        s1_re = s1[:256, :columns] - s1[256:, columns:]
        s1_im = s1[256:, :columns] + s1[:256, columns:]
        re = jnp.concatenate([s0[:128], s2[:128], s1_re], 0)
        im = jnp.concatenate([s0[128:], s2[128:], -s1_im[:128], s1_im[128:]], 0)
        high, low = halves(re * re + im * im)
        smooth = jnp.dot(band_ref[...], high, preferred_element_type=jnp.float32)
        smooth += jnp.dot(band_ref[...], low, preferred_element_type=jnp.float32)
        scale = lax.rsqrt(smooth * (1.0 / (2 * HALF + 1)) + EPS)
        re, im = re * scale, im * scale
        segments = pl.ds(n * together, together)
        for c, out_hbm in enumerate(outs_hbm):
            mine = slice(c * F // chunks, (c + 1) * F // chunks)
            for s in range(together):
                lanes = slice(s * LANES, (s + 1) * LANES)
                out_ref[n, c, :, s, 0] = re[mine, lanes].reshape(-1, rows, LANES)
                out_ref[n, c, :, s, 1] = im[mine, lanes].reshape(-1, rows, LANES)
            copy = pltpu.make_async_copy(out_ref.at[n, c], out_hbm.at[:, segments], out_sems.at[n, c])
            copy.start()
            done.append(copy)
    for copy in done:
        copy.wait()


def whiten(records, starts, rows, chunks):
    count = records.shape[1]
    parts = 4
    splits = 2 if count % 2 == 0 else 1
    per_chunk = F // chunks // rows
    tables = [jnp.asarray(t) for t in (hann_table(), *transform_tables())]
    return pl.pallas_call(
        whiten_kernel,
        in_specs=[
            pl.BlockSpec(memory_space=pltpu.SMEM),
            *[pl.BlockSpec(memory_space=pl.ANY) for _ in range(1 + len(tables))],
        ],
        out_specs=[pl.BlockSpec(memory_space=pl.ANY)] * chunks,
        out_shape=[jax.ShapeDtypeStruct((per_chunk, count, 2, rows, LANES), jnp.float32)] * chunks,
        scratch_shapes=[
            pltpu.VMEM(records.shape, jnp.float32),
            *[pltpu.VMEM(t.shape, jnp.float32) for t in tables],
            pltpu.VMEM((4, count * LANES, 256), jnp.float32),
            pltpu.VMEM((F, F), jnp.bfloat16),
            pltpu.VMEM((splits, chunks, per_chunk, count // splits, 2, rows, LANES), jnp.float32),
            pltpu.SemaphoreType.DMA((len(tables),)),
            pltpu.SemaphoreType.DMA((parts,)),
            pltpu.SemaphoreType.DMA((splits, chunks)),
        ],
        compiler_params=pltpu.CompilerParams(vmem_limit_bytes=56 << 20),
    )(starts, records, *tables)


def pair_kernel(index_ref, turn_ref, spectra_ref, out_ref, wide_ref, *, reach, turned):
    blocks, terms, _, rows, _ = spectra_ref.shape

    def build(i, carry):
        wide_ref[i, 0], wide_ref[i, 1] = halves(spectra_ref[i].reshape(-1, LANES))
        return carry

    lax.fori_loop(0, blocks, build, 0)
    ids = lax.broadcasted_iota(jnp.int32, (LANES, LANES), 0)

    def one_block(block, carry):
        pair_block(block, index_ref, turn_ref, spectra_ref, out_ref, wide_ref, ids, reach, turned)
        return carry

    lax.fori_loop(0, blocks, one_block, 0)


def pair_block(block, index_ref, turn_ref, spectra_ref, out_ref, wide_ref, ids, reach, turned):
    blocks, terms, _, rows, _ = spectra_ref.shape
    pairs = index_ref.shape[1]
    groups = out_ref.shape[1]
    share = pairs // groups
    span = 2 * reach + 1
    near = [lax.rem(block + (blocks - reach + j), blocks) for j in range(span)]
    left = jnp.concatenate([wide_ref[i, h] for i in near for h in range(2)], 1)

    def put(k, rows_here, re, im):
        z, q = k // share, k % share
        turn_re, turn_im = turn_ref[0, rows_here], turn_ref[1, rows_here]
        lanes = slice(q * LANES, (q + 1) * LANES)
        out_ref[block, z, 0, rows_here, lanes] = re * turn_re + im * turn_im
        out_ref[block, z, 1, rows_here, lanes] = im * turn_re - re * turn_im

    def by_product(ks):
        hots = []
        for j in range(span):
            wanted = [index_ref[block, k : k + 1, :] - j * LANES for k in ks]
            hot = [jnp.where(ids == w, 1.0, 0.0).astype(jnp.bfloat16) for w in wanted]
            hot = jnp.concatenate(hot, 1)
            hots += [hot, hot]
        found = jnp.dot(left, jnp.concatenate(hots, 0), preferred_element_type=jnp.float32)
        found = found.reshape(terms, 2, rows, -1)
        for i, k in enumerate(ks):
            lanes = slice(i * LANES, (i + 1) * LANES)
            re = im = 0
            for t in range(terms):
                partner_re, partner_im = found[t, 0, :, lanes], found[t, 1, :, lanes]
                own_re, own_im = spectra_ref[block, t, 0], spectra_ref[block, t, 1]
                re = re + (own_re * partner_re + own_im * partner_im)
                im = im + (own_im * partner_re - own_re * partner_im)
            put(k, slice(0, rows), re, im)

    def by_gather(k, first):
        row = jnp.broadcast_to(index_ref[block, k : k + 1, :], (8, LANES))
        lane, part = row & (LANES - 1), lax.shift_right_logical(row, 7)
        rows_here = slice(first, first + 8)
        re = im = 0
        for t in range(terms):
            partner = []
            for h in range(2):
                found = jnp.take_along_axis(spectra_ref[near[0], t, h, rows_here], lane, axis=1)
                for j in range(1, span):
                    other = jnp.take_along_axis(spectra_ref[near[j], t, h, rows_here], lane, axis=1)
                    found = jnp.where(part == j, other, found)
                partner.append(found)
            own_re = spectra_ref[block, t, 0, rows_here]
            own_im = spectra_ref[block, t, 1, rows_here]
            re = re + (own_re * partner[0] + own_im * partner[1])
            im = im + (own_im * partner[0] - own_re * partner[1])
        put(k, rows_here, re, im)

    chunks = [range(k, min(k + 2, pairs - turned)) for k in range(0, pairs - turned, 2)]
    gathers = [(k, first) for k in range(pairs - turned, pairs) for first in range(0, rows, 8)]
    for n, ks in enumerate(chunks):
        by_product(ks)
        for k, first in gathers[n * len(gathers) // len(chunks) : (n + 1) * len(gathers) // len(chunks)]:
            by_gather(k, first)


def pair_products(spectra, index, turn, groups, turned=6):
    blocks, terms, _, rows, _ = spectra.shape
    pairs = index.shape[1]
    reach = -(-REACH // LANES)
    shape = (groups, 2, rows, pairs // groups * LANES)
    return pl.pallas_call(
        functools.partial(pair_kernel, reach=reach, turned=turned),
        in_specs=[pl.BlockSpec(memory_space=pltpu.VMEM)] * 3,
        out_specs=pl.BlockSpec(memory_space=pltpu.VMEM),
        out_shape=jax.ShapeDtypeStruct((blocks, *shape), jnp.float32),
        scratch_shapes=[
            pltpu.VMEM((blocks, 2, terms * 2 * rows, LANES), jnp.bfloat16),
        ],
        compiler_params=pltpu.CompilerParams(vmem_limit_bytes=10 << 20),
        cost_estimate=pl.CostEstimate(
            flops=8 * (2 * reach + 1) * LANES * pairs * LANES * spectra.size // LANES,
            bytes_accessed=8 * spectra.size,
            transcendentals=0,
        ),
    )(index, turn, spectra)


def lag_kernel(cross_ref, tables_ref, *rest):
    earlier_ref = rest[0] if len(rest) == 4 else None
    last = len(rest) > 1
    out_ref = rest[-2] if last else rest[0]
    bins = cross_ref.shape[0] * cross_ref.shape[2]
    half = LAGS // 2
    mirror = LANES - 1 - lax.broadcasted_iota(jnp.int32, (LANES, LANES), 1)

    def transform(x, first):
        high, low = halves(x)
        total = dot_tn(high, tables_ref[first + 1]) + dot_tn(low, tables_ref[first])
        return total + dot_tn(high, tables_ref[first])

    done = []
    for i in range(out_ref.shape[0]):
        lanes = slice(i * LANES, (i + 1) * LANES)
        re = cross_ref[:, 0, :, lanes].reshape(bins, LANES)
        im = cross_ref[:, 1, :, lanes].reshape(bins, LANES)
        even = transform(re, 0)
        odd = transform(im, 2)
        pieces = [(half, even - odd)]
        before = even + odd
        for first in range(0, half, LANES):
            turned = jnp.take_along_axis(before[:, first : first + LANES], mirror, axis=1)
            pieces.append((half - first - LANES, turned))
        for first, x in pieces:
            at = slice(first, first + x.shape[1])
            out_ref[i, :, at] = x if earlier_ref is None else x + earlier_ref[i, :, at]
        if last:
            done.append(pltpu.make_async_copy(out_ref.at[i], rest[-3].at[i], rest[-1].at[i]))
            done[i].start()
    for copy in done:
        copy.wait()


def lag_transform(cross, tables, earlier, last):
    count = cross.shape[3] // LANES
    given = [cross, jnp.asarray(tables)]
    if earlier is not None:
        given.append(earlier)
    shape = (count, LANES, LAGS)
    return pl.pallas_call(
        lag_kernel,
        in_specs=[pl.BlockSpec(memory_space=pltpu.VMEM)] * len(given),
        out_specs=pl.BlockSpec(memory_space=pl.ANY if last else pltpu.VMEM),
        out_shape=jax.ShapeDtypeStruct(shape, jnp.float32),
        scratch_shapes=[pltpu.VMEM(shape, jnp.float32), pltpu.SemaphoreType.DMA((count,))] if last else [],
        compiler_params=pltpu.CompilerParams(vmem_limit_bytes=10 << 20),
        cost_estimate=pl.CostEstimate(
            flops=6 * LAGS * cross.size, bytes_accessed=8 * cross.size, transcendentals=0
        ),
    )(*given)


def local(records, starts, offsets):
    axes = ("blk", "inner")
    blocks, groups = lax.axis_size("blk"), lax.axis_size("inner")
    devices = blocks * groups
    here, count = records.shape[:2]
    ids = jnp.arange(here, dtype=jnp.int32)[:, None] + REACH
    index = lax.all_gather((ids + offsets).T, "blk", axis=0)
    chunks = 2 if F // devices % 16 == 0 else 1
    width = F // devices // chunks
    rows = max(width, 8)
    split = rows // width
    tables = lag_tables(count * groups)
    device = lax.axis_index("blk") * groups + lax.axis_index("inner")
    turns = lax.dynamic_index_in_dim(turn_table(devices, width, rows, chunks), device, 1, keepdims=False)
    turns = jnp.broadcast_to(turns, (*turns.shape[:3], LANES))
    lags = None
    spectra = []
    for white in whiten(records, starts, rows, chunks):
        white = white.reshape(-1, count // split, split, 2, split, width, LANES)
        white = white.transpose(0, 4, 1, 3, 2, 5, 6).reshape(devices, -1, LANES)
        white = lax.all_to_all(white, axes, 0, 0, tiled=True)
        spectra.append(white.reshape(blocks, -1, 2, rows, LANES))
    for c in range(chunks):
        cross = pair_products(spectra[c], index, turns[c], groups)
        if split > 1:
            cross = cross.reshape(blocks, groups, 2, split, width, -1).sum(3)
        cross = lax.all_to_all(cross.reshape(devices, 2 * width, -1), axes, 0, 0, tiled=True)
        cross = cross.reshape(devices, 2, width, -1)
        if split > 1:
            cross = cross.transpose(1, 0, 2, 3).reshape(1, 2, F // chunks, -1)
        mine = tables[:, c * F // chunks : (c + 1) * F // chunks]
        lags = lag_transform(cross, mine, lags, c == chunks - 1)
    return lags


def solution(mesh):
    placed = (P("blk", "inner", None), P("inner"), P("blk", None))
    return jax.shard_map(
        local, mesh=mesh, in_specs=placed, out_specs=P("inner", "blk", None), check_vma=False
    )
```

```python
import functools
import math

import jax
import jax.numpy as jnp
import numpy as np
from jax import lax
from jax.experimental import pallas as pl
from jax.experimental.pallas import tpu as pltpu
from jax.sharding import PartitionSpec as P

SEG = 1024
LAGS = 768
HALF = 32
REACH = 256
F = 512
LANES = 128
EPS = 1e-06


def bin_order():
    m = np.arange(128)
    return np.concatenate([4 * m, 4 * m + 2, 4 * m + 1, 4 * m[::-1] + 3])


def transform_tables():
    u = np.arange(256)

    def parts(bins, sign):
        angle = 2 * np.pi / SEG * (bins[:, None] * u[None, :] % SEG)
        return np.concatenate([np.cos(angle), sign * np.sin(angle)], 0).astype(np.float32)

    m = np.arange(256)
    return parts(4 * m[:128], -1), parts(4 * m[:128] + 2, -1), parts(4 * m + 1, 1)


def lag_tables(segment_count):
    bins = bin_order()[:, None]
    angle = 2 * np.pi / SEG * bins * (np.arange(LAGS // 2)[None, :] + 0.5)
    factor = math.sqrt(segment_count / F) / segment_count
    tables = []
    for table in (np.cos(angle) * factor, np.sin(angle) * factor):
        high = table.astype(jnp.bfloat16)
        tables += [high, (table - high.astype(np.float64)).astype(jnp.bfloat16)]
    return np.stack(tables)


def turn_table(devices, width, rows, chunks):
    half = np.pi / SEG * bin_order().reshape(chunks, devices, 1, 1, width, 1)
    half = np.broadcast_to(half, (chunks, devices, 1, rows // width, width, 1))
    table = np.concatenate([np.cos(half), np.sin(half)], 2)
    return jnp.asarray(table.reshape(chunks, devices, 2, rows, 1).astype(np.float32))


def halves(x):
    high = x.astype(jnp.bfloat16)
    return high, (x - high.astype(jnp.float32)).astype(jnp.bfloat16)


def dot_nt(a, b, precision=None):
    return lax.dot_general(
        a, b, (((1,), (1,)), ((), ())), precision=precision, preferred_element_type=jnp.float32
    )


def dot_tn(a, b):
    return lax.dot_general(a, b, (((0,), (0,)), ((), ())), preferred_element_type=jnp.float32)


def hann_table():
    window = 0.5 - 0.5 * np.cos(2 * np.pi / SEG * np.arange(SEG))
    return np.tile(window[None, :], (8, 1)).astype(np.float32)


def whiten_kernel(
    starts_ref, records_hbm, hann_hbm, even0_hbm, even2_hbm, odd_hbm, *rest
):
    *outs_hbm, records_ref, hann_ref, even0_ref, even2_ref, odd_ref, folded_ref, band_ref = rest[:-4]
    out_ref, table_sems, record_sems, out_sems = rest[-4:]
    here, count = records_ref.shape[:2]
    rows = out_ref.shape[5]
    parts, (halves_out, chunks) = record_sems.shape[0], out_sems.shape
    part, together = here // parts, count // halves_out
    columns = together * LANES

    tables = [(hann_hbm, hann_ref), (even0_hbm, even0_ref), (even2_hbm, even2_ref), (odd_hbm, odd_ref)]
    tables = [pltpu.make_async_copy(s, d, table_sems.at[i]) for i, (s, d) in enumerate(tables)]
    pieces = [pl.ds(p * part, part) for p in range(parts)]
    pieces = [
        pltpu.make_async_copy(records_hbm.at[at], records_ref.at[at], record_sems.at[p])
        for p, at in enumerate(pieces)
    ]
    for copy in [tables[0], *pieces, *tables[1:]]:
        copy.start()

    def bins(axis):
        p = lax.broadcasted_iota(jnp.int32, (F, F), axis)
        even = jnp.where(p < 128, 4 * p, 4 * p - 510)
        return jnp.where(p < 256, even, jnp.where(p < 384, 4 * p - 1023, 2047 - 4 * p))

    distance = jnp.abs(bins(0) - bins(1))
    distance = jnp.minimum(distance, F - distance)
    band_ref[...] = jnp.where(distance <= HALF, 1.0, 0.0).astype(jnp.bfloat16)

    samples = lax.broadcasted_iota(jnp.int32, (8, SEG), 1)
    tables[0].wait()
    windows = []
    for s in range(count):
        begin = starts_ref[s]
        window = pltpu.roll(hann_ref[...], lax.rem(begin, SEG), 1)[:1]
        early = jnp.where(samples >= begin, 1.0, 0.0)[:1] * window
        windows.append((early, window - early))
    for p, copy in enumerate(pieces):
        copy.wait()
        for s, (early, late) in enumerate(windows):
            at = slice(p * part, (p + 1) * part)
            x = records_ref[at, s, :SEG] * early + records_ref[at, s, SEG:] * late
            x = [x[:, 256 * j : 256 * (j + 1)] for j in range(4)]
            at = slice(s * LANES + p * part, s * LANES + (p + 1) * part)
            folded_ref[0, at, :] = (x[0] + x[2]) + (x[1] + x[3])
            folded_ref[1, at, :] = (x[0] + x[2]) - (x[1] + x[3])
            folded_ref[2, at, :] = x[0] - x[2]
            folded_ref[3, at, :] = x[1] - x[3]

    for copy in tables[1:]:
        copy.wait()
    highest = lax.Precision.HIGHEST
    done = []
    for n in range(halves_out):
        at = slice(n * columns, (n + 1) * columns)
        s0 = dot_nt(even0_ref[...], folded_ref[0, at, :], highest)
        s2 = dot_nt(even2_ref[...], folded_ref[1, at, :], highest)
        odd = jnp.concatenate([folded_ref[2, at, :], folded_ref[3, at, :]], 0)
        s1 = dot_nt(odd_ref[...], odd, highest)
        s1_re = s1[:256, :columns] - s1[256:, columns:]
        s1_im = s1[256:, :columns] + s1[:256, columns:]
        re = jnp.concatenate([s0[:128], s2[:128], s1_re], 0)
        im = jnp.concatenate([s0[128:], s2[128:], -s1_im[:128], s1_im[128:]], 0)
        high, low = halves(re * re + im * im)
        smooth = jnp.dot(band_ref[...], high, preferred_element_type=jnp.float32)
        smooth += jnp.dot(band_ref[...], low, preferred_element_type=jnp.float32)
        scale = lax.rsqrt(smooth * (1.0 / (2 * HALF + 1)) + EPS)
        re, im = re * scale, im * scale
        segments = pl.ds(n * together, together)
        for c, out_hbm in enumerate(outs_hbm):
            mine = slice(c * F // chunks, (c + 1) * F // chunks)
            for s in range(together):
                lanes = slice(s * LANES, (s + 1) * LANES)
                out_ref[n, c, :, s, 0] = re[mine, lanes].reshape(-1, rows, LANES)
                out_ref[n, c, :, s, 1] = im[mine, lanes].reshape(-1, rows, LANES)
            copy = pltpu.make_async_copy(out_ref.at[n, c], out_hbm.at[:, segments], out_sems.at[n, c])
            copy.start()
            done.append(copy)
    for copy in done:
        copy.wait()


def whiten(records, starts, rows, chunks):
    count = records.shape[1]
    parts = 4
    splits = 1
    per_chunk = F // chunks // rows
    tables = [jnp.asarray(t) for t in (hann_table(), *transform_tables())]
    return pl.pallas_call(
        whiten_kernel,
        in_specs=[
            pl.BlockSpec(memory_space=pltpu.SMEM),
            *[pl.BlockSpec(memory_space=pl.ANY) for _ in range(1 + len(tables))],
        ],
        out_specs=[pl.BlockSpec(memory_space=pl.ANY)] * chunks,
        out_shape=[jax.ShapeDtypeStruct((per_chunk, count, 2, rows, LANES), jnp.float32)] * chunks,
        scratch_shapes=[
            pltpu.VMEM(records.shape, jnp.float32),
            *[pltpu.VMEM(t.shape, jnp.float32) for t in tables],
            pltpu.VMEM((4, count * LANES, 256), jnp.float32),
            pltpu.VMEM((F, F), jnp.bfloat16),
            pltpu.VMEM((splits, chunks, per_chunk, count // splits, 2, rows, LANES), jnp.float32),
            pltpu.SemaphoreType.DMA((len(tables),)),
            pltpu.SemaphoreType.DMA((parts,)),
            pltpu.SemaphoreType.DMA((splits, chunks)),
        ],
        compiler_params=pltpu.CompilerParams(vmem_limit_bytes=56 << 20),
    )(starts, records, *tables)


def pair_kernel(index_ref, turn_ref, spectra_ref, out_ref, wide_ref, *, reach, turned):
    blocks, terms, _, rows, _ = spectra_ref.shape

    def build(i, carry):
        wide_ref[i, 0], wide_ref[i, 1] = halves(spectra_ref[i].reshape(-1, LANES))
        return carry

    lax.fori_loop(0, blocks, build, 0)
    ids = lax.broadcasted_iota(jnp.int32, (LANES, LANES), 0)

    def one_block(block, carry):
        pair_block(block, index_ref, turn_ref, spectra_ref, out_ref, wide_ref, ids, reach, turned)
        return carry

    lax.fori_loop(0, blocks, one_block, 0)


def pair_block(block, index_ref, turn_ref, spectra_ref, out_ref, wide_ref, ids, reach, turned):
    blocks, terms, _, rows, _ = spectra_ref.shape
    pairs = index_ref.shape[1]
    groups = out_ref.shape[1]
    share = pairs // groups
    span = 2 * reach + 1
    near = [lax.rem(block + (blocks - reach + j), blocks) for j in range(span)]
    left = jnp.concatenate([wide_ref[i, h] for i in near for h in range(2)], 1)

    def put(k, rows_here, re, im):
        z, q = k // share, k % share
        turn_re, turn_im = turn_ref[0, rows_here], turn_ref[1, rows_here]
        lanes = slice(q * LANES, (q + 1) * LANES)
        out_ref[block, z, 0, rows_here, lanes] = re * turn_re + im * turn_im
        out_ref[block, z, 1, rows_here, lanes] = im * turn_re - re * turn_im

    def by_product(ks):
        hots = []
        for j in range(span):
            wanted = [index_ref[block, k : k + 1, :] - j * LANES for k in ks]
            hot = [jnp.where(ids == w, 1.0, 0.0).astype(jnp.bfloat16) for w in wanted]
            hot = jnp.concatenate(hot, 1)
            hots += [hot, hot]
        found = jnp.dot(left, jnp.concatenate(hots, 0), preferred_element_type=jnp.float32)
        found = found.reshape(terms, 2, rows, -1)
        for i, k in enumerate(ks):
            lanes = slice(i * LANES, (i + 1) * LANES)
            re = im = 0
            for t in range(terms):
                partner_re, partner_im = found[t, 0, :, lanes], found[t, 1, :, lanes]
                own_re, own_im = spectra_ref[block, t, 0], spectra_ref[block, t, 1]
                re = re + (own_re * partner_re + own_im * partner_im)
                im = im + (own_im * partner_re - own_re * partner_im)
            put(k, slice(0, rows), re, im)

    def by_gather(k, first):
        row = jnp.broadcast_to(index_ref[block, k : k + 1, :], (8, LANES))
        lane, part = row & (LANES - 1), lax.shift_right_logical(row, 7)
        rows_here = slice(first, first + 8)
        re = im = 0
        for t in range(terms):
            partner = []
            for h in range(2):
                found = jnp.take_along_axis(spectra_ref[near[0], t, h, rows_here], lane, axis=1)
                for j in range(1, span):
                    other = jnp.take_along_axis(spectra_ref[near[j], t, h, rows_here], lane, axis=1)
                    found = jnp.where(part == j, other, found)
                partner.append(found)
            own_re = spectra_ref[block, t, 0, rows_here]
            own_im = spectra_ref[block, t, 1, rows_here]
            re = re + (own_re * partner[0] + own_im * partner[1])
            im = im + (own_im * partner[0] - own_re * partner[1])
        put(k, rows_here, re, im)

    chunks = [range(k, min(k + 2, pairs - turned)) for k in range(0, pairs - turned, 2)]
    gathers = [(k, first) for k in range(pairs - turned, pairs) for first in range(0, rows, 8)]
    for n, ks in enumerate(chunks):
        by_product(ks)
        for k, first in gathers[n * len(gathers) // len(chunks) : (n + 1) * len(gathers) // len(chunks)]:
            by_gather(k, first)


def pair_products(spectra, index, turn, groups, turned=6):
    blocks, terms, _, rows, _ = spectra.shape
    pairs = index.shape[1]
    reach = -(-REACH // LANES)
    shape = (groups, 2, rows, pairs // groups * LANES)
    return pl.pallas_call(
        functools.partial(pair_kernel, reach=reach, turned=turned),
        in_specs=[pl.BlockSpec(memory_space=pltpu.VMEM)] * 3,
        out_specs=pl.BlockSpec(memory_space=pltpu.VMEM),
        out_shape=jax.ShapeDtypeStruct((blocks, *shape), jnp.float32),
        scratch_shapes=[
            pltpu.VMEM((blocks, 2, terms * 2 * rows, LANES), jnp.bfloat16),
        ],
        compiler_params=pltpu.CompilerParams(vmem_limit_bytes=10 << 20),
        cost_estimate=pl.CostEstimate(
            flops=8 * (2 * reach + 1) * LANES * pairs * LANES * spectra.size // LANES,
            bytes_accessed=8 * spectra.size,
            transcendentals=0,
        ),
    )(index, turn, spectra)


def lag_kernel(cross_ref, tables_ref, *rest):
    earlier_ref = rest[0] if len(rest) == 4 else None
    last = len(rest) > 1
    out_ref = rest[-2] if last else rest[0]
    bins = cross_ref.shape[0] * cross_ref.shape[2]
    half = LAGS // 2
    mirror = LANES - 1 - lax.broadcasted_iota(jnp.int32, (LANES, LANES), 1)

    def transform(x, first):
        high, low = halves(x)
        total = dot_tn(high, tables_ref[first + 1]) + dot_tn(low, tables_ref[first])
        return total + dot_tn(high, tables_ref[first])

    done = []
    for i in range(out_ref.shape[0]):
        lanes = slice(i * LANES, (i + 1) * LANES)
        re = cross_ref[:, 0, :, lanes].reshape(bins, LANES)
        im = cross_ref[:, 1, :, lanes].reshape(bins, LANES)
        even = transform(re, 0)
        odd = transform(im, 2)
        pieces = [(half, even - odd)]
        before = even + odd
        for first in range(0, half, LANES):
            turned = jnp.take_along_axis(before[:, first : first + LANES], mirror, axis=1)
            pieces.append((half - first - LANES, turned))
        for first, x in pieces:
            at = slice(first, first + x.shape[1])
            out_ref[i, :, at] = x if earlier_ref is None else x + earlier_ref[i, :, at]
        if last:
            done.append(pltpu.make_async_copy(out_ref.at[i], rest[-3].at[i], rest[-1].at[i]))
            done[i].start()
    for copy in done:
        copy.wait()


def lag_transform(cross, tables, earlier, last):
    count = cross.shape[3] // LANES
    given = [cross, jnp.asarray(tables)]
    if earlier is not None:
        given.append(earlier)
    shape = (count, LANES, LAGS)
    return pl.pallas_call(
        lag_kernel,
        in_specs=[pl.BlockSpec(memory_space=pltpu.VMEM)] * len(given),
        out_specs=pl.BlockSpec(memory_space=pl.ANY if last else pltpu.VMEM),
        out_shape=jax.ShapeDtypeStruct(shape, jnp.float32),
        scratch_shapes=[pltpu.VMEM(shape, jnp.float32), pltpu.SemaphoreType.DMA((count,))] if last else [],
        compiler_params=pltpu.CompilerParams(vmem_limit_bytes=10 << 20),
        cost_estimate=pl.CostEstimate(
            flops=6 * LAGS * cross.size, bytes_accessed=8 * cross.size, transcendentals=0
        ),
    )(*given)


def local(records, starts, offsets):
    axes = ("blk", "inner")
    blocks, groups = lax.axis_size("blk"), lax.axis_size("inner")
    devices = blocks * groups
    here, count = records.shape[:2]
    ids = jnp.arange(here, dtype=jnp.int32)[:, None] + REACH
    index = lax.all_gather((ids + offsets).T, "blk", axis=0)
    chunks = 2 if F // devices % 16 == 0 else 1
    width = F // devices // chunks
    rows = max(width, 8)
    split = rows // width
    tables = lag_tables(count * groups)
    device = lax.axis_index("blk") * groups + lax.axis_index("inner")
    turns = lax.dynamic_index_in_dim(turn_table(devices, width, rows, chunks), device, 1, keepdims=False)
    turns = jnp.broadcast_to(turns, (*turns.shape[:3], LANES))
    lags = None
    spectra = []
    for white in whiten(records, starts, rows, chunks):
        white = white.reshape(-1, count // split, split, 2, split, width, LANES)
        white = white.transpose(0, 4, 1, 3, 2, 5, 6).reshape(devices, -1, LANES)
        white = lax.all_to_all(white, axes, 0, 0, tiled=True)
        spectra.append(white.reshape(blocks, -1, 2, rows, LANES))
    for c in range(chunks):
        cross = pair_products(spectra[c], index, turns[c], groups)
        if split > 1:
            cross = cross.reshape(blocks, groups, 2, split, width, -1).sum(3)
        cross = lax.all_to_all(cross.reshape(devices, 2 * width, -1), axes, 0, 0, tiled=True)
        cross = cross.reshape(devices, 2, width, -1)
        if split > 1:
            cross = cross.transpose(1, 0, 2, 3).reshape(1, 2, F // chunks, -1)
        mine = tables[:, c * F // chunks : (c + 1) * F // chunks]
        lags = lag_transform(cross, mine, lags, c == chunks - 1)
    return lags


def solution(mesh):
    placed = (P("blk", "inner", None), P("inner"), P("blk", None))
    return jax.shard_map(
        local, mesh=mesh, in_specs=placed, out_specs=P("inner", "blk", None), check_vma=False
    )
```
